512 devices in a mesh: dp: 8 (over y), fsdp: 64 (over x, z, core).
Axes of the slice: x: 4, y: 8, z: 8, core: 2. Of those that a mesh axis runs over, the one named last changes fastest.
Arguments:
- gradients: bfloat16 [8, 256, 512, 512], P('dp', None, 'fsdp')
- statistics: float32 [512, 512, 512], P(('dp', 'fsdp')), as said below
- newton_steps: int32 [512], P(('dp', 'fsdp')), may hold values from 1 to 3, as said below
- second_moment: float32 [256, 512, 512], P('dp', 'fsdp'), may hold values from 0.01 to 1
Outputs:
- update: bfloat16 [256, 512, 512], P('dp', 'fsdp')
- new_moment: float32 [256, 512, 512], P('dp', 'fsdp')
The draws below stay inside these ranges and needn't reach their ends.
Inputs may be any that keep to these rules, and one draw needn't show every extreme that they name: `newton_steps`: each factor takes 1, 2 or 3 iterations; about half take one; some factor takes 3 and some takes 1 in every draw. `statistics`: each matrix is symmetric with a positive diagonal and strictly dominant diagonal after symmetric scaling.
All inputs are finite; a program needn't handle non-finite values.
Results may differ from the reference program's by a relative error of at most 0.002.
The reference program's roundings to bfloat16 on the way count: a program that leaves them out, or rounds other values in their place, can miss the bound.
Values may be sent and summed in bfloat16 or wider, within the bound.
A program may use at most 64 MiB of HBM per device.

```python
import math
import jax
import jax.numpy as jnp
from jax import lax

BS = 512
NB = 256
NF = 512
N_DP = 8


def draw_gradients(key, part):
    key = jax.random.fold_in(key, 11)
    keys = jax.random.split(key, 5)
    position = jnp.arange(BS, dtype=jnp.float32) / (BS - 1)
    trend = 30.0 ** position
    base = jax.random.normal(keys[0], (N_DP, NB, BS, BS), jnp.float32)
    pairing = jax.random.permutation(keys[4], N_DP)
    group = jnp.arange(NB, dtype=jnp.int32) // (NB // N_DP)
    spike = 1.0 + 2.0 * (pairing[:, None] == group[None, :]).astype(jnp.float32)
    row_scale = trend[None, :] * jnp.exp(jax.random.uniform(keys[1], (NB, BS), jnp.float32, 0.0, math.log(2.0)))
    col_scale = jnp.exp(jax.random.uniform(keys[2], (NB, BS), jnp.float32, 0.0, math.log(3.2)))
    values = base * spike[:, :, None, None] * row_scale[None, :, :, None] * col_scale[None, :, None, :]
    return values.astype(jnp.bfloat16)


def draw_statistics(key, part):
    key = jax.random.fold_in(key, 12)
    keys = jax.random.split(key, 2)
    diagonal = BS * jnp.exp(jax.random.uniform(keys[0], (NF, BS), jnp.float32, 0.0, math.log(3000.0)))
    noise = jax.random.uniform(keys[1], (NF, BS, BS), jnp.float32, -1.0, 1.0)
    symmetric = 0.5 * (noise + jnp.swapaxes(noise, 1, 2))
    identity = jnp.eye(BS, dtype=jnp.float32)
    core = identity[None] + (1.0 - identity[None]) * symmetric * (0.9 / (BS - 1))
    root_diag = jnp.sqrt(diagonal)
    return core * root_diag[:, :, None] * root_diag[:, None, :]


def draw_newton_steps(key, part):
    key = jax.random.fold_in(key, 13)
    keys = jax.random.split(key, 3)
    raw_value = jax.random.randint(keys[0], (NF,), 0, 8)
    steps_drawn = (1 + (raw_value >= 4).astype(jnp.int32) + (raw_value >= 7).astype(jnp.int32)).astype(jnp.int32)
    highest = jax.random.randint(keys[1], (), 0, NF)
    steps_drawn = steps_drawn.at[highest].set(3)
    lowest = (highest + 1 + jax.random.randint(keys[2], (), 0, NF - 1)) % NF
    steps_drawn = steps_drawn.at[lowest].set(1)
    return steps_drawn.astype(jnp.int32)


def levels(rng, extent, cuts, low, largest):
    def one(dim, shards_of):
        heights = jax.random.uniform(jax.random.fold_in(jax.random.fold_in(rng, 6), dim), (shards_of,), jnp.float32, low / len(cuts), largest / len(cuts))
        return jnp.repeat(jnp.exp(heights), extent[dim] // shards_of).reshape((-1,) + (1,) * (len(extent) - dim - 1))

    factor_of = one(*cuts[0])
    for cut in cuts[1:]:
        factor_of = factor_of * one(*cut)
    return factor_of


def setup_inputs(seed: int = 0) -> dict:
    streams_of = jax.random.split(jax.random.key(seed), 5)
    gradients = draw_gradients(jax.random.fold_in(streams_of[4], 71), 0)
    statistics = draw_statistics(jax.random.fold_in(streams_of[4], 71), 0)
    newton_steps = draw_newton_steps(jax.random.fold_in(streams_of[4], 71), 0)
    second_moment = jnp.clip(jnp.exp(math.log(1.0) - 4.6051702 * jax.random.uniform(streams_of[3], (NB, BS, BS), jnp.float32) ** levels(streams_of[3], (NB, BS, BS), ((0, 8), (1, 64)), -0.2, 0.2)), 0.01, 1.0)
    return {"gradients": gradients, "statistics": statistics, "newton_steps": newton_steps, "second_moment": second_moment}


stat_decay = 0.9
moment_decay = 0.95
adam_eps = 1e-08
ratio_eps = 1e-06
HIGH = lax.Precision.HIGHEST

def inverse_root(statistic, step_count):
    identity = jnp.eye(statistic.shape[0], dtype=jnp.float32)
    frobenius = jnp.sqrt(jnp.sum(statistic * statistic))
    scaling = 5.0 / (2.0 * frobenius)
    start = (jnp.sqrt(jnp.sqrt(scaling)) * identity, scaling * statistic)

    def one_step(counter, state_pair):
        iterate, moment_m = state_pair
        factor = (5.0 * identity - moment_m) / 4.0
        iterate = jnp.dot(iterate, factor, precision=HIGH)
        square = jnp.dot(factor, factor, precision=HIGH)
        fourth = jnp.dot(square, square, precision=HIGH)
        moment_m = jnp.dot(fourth, moment_m, precision=HIGH)
        return (iterate, moment_m)
    iterate, moment_m = lax.fori_loop(0, step_count, one_step, start)
    return iterate.astype(jnp.bfloat16)

def reference(gradients, statistics, newton_steps, second_moment):
    summed = gradients[0].astype(jnp.float32)
    for replica in range(1, N_DP):
        summed = summed + gradients[replica].astype(jnp.float32)
    grad_mean = summed / N_DP
    grad_bf = grad_mean.astype(jnp.bfloat16)

    def factor_root(factor_index):
        block = grad_bf[factor_index // 2]
        chosen = jnp.where(factor_index % 2 == 0, block, block.T)
        gram = jnp.dot(chosen, chosen.T, preferred_element_type=jnp.float32)
        statistic = stat_decay * statistics[factor_index] + (1.0 - stat_decay) * gram
        return inverse_root(statistic, newton_steps[factor_index])
    roots = lax.map(factor_root, jnp.arange(NF, dtype=jnp.int32))

    def precondition(block_index):
        middle = jnp.dot(roots[2 * block_index], grad_bf[block_index], preferred_element_type=jnp.float32).astype(jnp.bfloat16)
        return jnp.dot(middle, roots[2 * block_index + 1], preferred_element_type=jnp.float32).astype(jnp.bfloat16)
    direction = lax.map(precondition, jnp.arange(NB, dtype=jnp.int32))
    new_moment = moment_decay * second_moment + (1.0 - moment_decay) * grad_mean * grad_mean
    adam = grad_mean / (jnp.sqrt(new_moment) + adam_eps)
    dir_wide = direction.astype(jnp.float32)
    adam_sq = lax.optimization_barrier(jnp.sum(adam * adam, axis=(1, 2)))
    dir_sq = lax.optimization_barrier(jnp.sum(dir_wide * dir_wide, axis=(1, 2)))
    ratio = jnp.sqrt(adam_sq) / (jnp.sqrt(dir_sq) + ratio_eps)
    update = (dir_wide * ratio[:, None, None]).astype(jnp.bfloat16)
    return (update, new_moment)
```

```python
import functools

import jax
import jax.numpy as jnp
from jax import lax
from jax.experimental import pallas as pl
from jax.experimental.pallas import tpu as pltpu
from jax.sharding import PartitionSpec as P

stat_decay = 0.9
moment_decay = 0.95
adam_eps = 1e-08
ratio_eps = 1e-06
MESH = pl.DeviceIdType.MESH
F32 = jnp.float32
BF16 = jnp.bfloat16
LANES = 128
ROWS = 8
TILE = 64
SIZE = 512
WAYS = 8
COLS = 4
RINGS = 8
OWNERS = 64
HALF = OWNERS // 2
MSG = 48


def kernel(
    grad, stats, steps, second, upd, moment,
    own, stat_v, second_v, moment_v,
    r1, leaf, r2, s2, s3, r3, r4,
    outgoing, gathered, block, middle, direction, back, roots,
    a_f, p_f, q_f, r_f, m_f, x_f,
    a_l, b_l, m_l, x_l, t_r, u_r,
    local_sem, ring_send, ring_recv, row_send, row_recv, root_send, root_recv, back_send, back_recv,
):
    y = lax.axis_index("dp")
    me = lax.axis_index("fsdp")
    core = lax.rem(me, 2)
    chip = lax.div(me, 2)
    z = lax.rem(chip, RINGS)

    own_copy = pltpu.make_async_copy(grad, own, local_sem.at[0])
    stat_copy = pltpu.make_async_copy(stats, stat_v, local_sem.at[1])
    second_copy = pltpu.make_async_copy(second, second_v, local_sem.at[2])
    own_copy.start()

    barrier = pltpu.get_barrier_semaphore()
    for shift in (1, WAYS - 1):
        pl.semaphore_signal(
            barrier, inc=1, device_id={"dp": lax.rem(y + shift, WAYS)}, device_id_type=MESH
        )

    def greet(offset, carry):
        pl.semaphore_signal(
            barrier, inc=1, device_id={"fsdp": lax.rem(me + offset, OWNERS)}, device_id_type=MESH
        )
        return carry

    lax.fori_loop(1, OWNERS, greet, 0)
    stat_copy.start()
    second_copy.start()
    pl.semaphore_wait(barrier, OWNERS + 1)

    def group(way, distance):
        return lax.rem(y + (distance if way == 0 else WAYS - distance), WAYS)

    def column(place):
        half = lax.div(place + 1, 2)
        return lax.rem(z + 4 + half * (1 - 2 * lax.rem(place, 2)) + RINGS, RINGS)

    def ring(way, index, source, target):
        return pltpu.make_async_remote_copy(
            src_ref=source,
            dst_ref=target,
            send_sem=ring_send.at[way, index],
            recv_sem=ring_recv.at[way, index],
            device_id={"dp": group(way, 1)},
            device_id_type=MESH,
        )

    def mine(way, distance, place):
        return own[group(way, distance), :, column(place)].astype(F32)

    def hop1(way, j):
        place = j + 4 * way
        return ring(way, j, grad.at[group(way, 4), :, column(place)], r1.at[way, j])

    def hop2_leaf(way, j):
        place = j + 4 * (1 - way)
        return ring(way, 4 + j, grad.at[group(way, 3), :, column(place)], leaf.at[way, j])

    def hop2(way, j):
        return ring(way, 8 + j, s2.at[way, j], r2.at[way, j])

    def hop3(way, j):
        return ring(way, 12 + j, r2.at[way, j], r3.at[way, j + 4 * way])

    def hop3_leaf(way, j):
        return ring(way, 16 + j, s3.at[way, j], r3.at[way, j + 4 * (1 - way)])

    def hop4(way, place):
        return ring(way, 20 + place, r3.at[way, place], r4.at[way, place])

    def each(count, fn):
        def one(j, carry):
            fn(j)
            return carry

        lax.fori_loop(0, count, one, 0)

    def start1(j):
        hop1(0, j).start()
        hop1(1, j).start()

    def start2_leaf(j):
        hop2_leaf(0, j).start()
        hop2_leaf(1, j).start()

    each(4, start1)
    each(4, start2_leaf)
    own_copy.wait()

    def start2(j):
        for way in (0, 1):
            hop1(way, j).wait_recv()
            s2[way, j] = r1[way, j].astype(F32) + mine(way, 3, j + 4 * way)
            hop2(way, j).start()

    each(4, start2)

    def long3(way, j):
        hop2(way, j).wait_recv()
        r2[way, j] = r2[way, j] + mine(way, 2, j + 4 * way)
        hop3(way, j).start()

    def short3(way, j):
        hop2_leaf(way, j).wait_recv()
        s3[way, j] = leaf[way, j].astype(F32) + mine(way, 2, j + 4 * (1 - way))
        hop3_leaf(way, j).start()

    def start3_low(j):
        short3(1, j)
        long3(0, j)

    def start3_high(j):
        short3(0, j)
        long3(1, j)

    each(4, start3_low)
    each(4, start3_high)

    def step4(way, place, arrival):
        arrival.wait_recv()
        r3[way, place] = r3[way, place] + mine(way, 1, place)
        hop4(way, place).start()

    def start4_low(j):
        step4(0, j, hop3(0, j))
        step4(1, j, hop3_leaf(1, j))

    def start4_high(j):
        step4(0, j + 4, hop3_leaf(0, j))
        step4(1, j + 4, hop3(1, j))

    each(4, start4_low)
    each(4, start4_high)
    second_copy.wait()

    def rows_to(target, source):
        return pltpu.make_async_remote_copy(
            src_ref=source,
            dst_ref=gathered.at[me],
            send_sem=row_send,
            recv_sem=row_recv,
            device_id={"fsdp": target},
            device_id_type=MESH,
        )

    sublane = lax.broadcasted_iota(jnp.int32, (COLS, 16, LANES), 1)

    def finish(place):
        hop4(0, place).wait_recv()
        hop4(1, place).wait_recv()
        col = column(place)
        total = r4[0, place] + r4[1, place] + own[y, :, col].astype(F32)
        mean = total * (1.0 / WAYS)
        new = moment_decay * second_v[:, col] + (1.0 - moment_decay) * mean * mean
        moment_v[:, col] = new
        adam = mean / (jnp.sqrt(new) + adam_eps)
        square = adam * adam
        parts = [mean[:, :, c * LANES:(c + 1) * LANES] for c in range(4)]
        squares = [square[:, :, c * LANES:(c + 1) * LANES] for c in range(4)]
        lanes = jnp.sum((squares[0] + squares[1]) + (squares[2] + squares[3]), axis=1, keepdims=True)
        high = lanes.astype(BF16).astype(F32)
        rest = lanes - high
        mid = rest.astype(BF16).astype(F32)
        low = rest - mid
        extra = jnp.where(
            sublane == 0, high, jnp.where(sublane == 1, mid, jnp.where(sublane == 2, low, 0.0))
        )
        outgoing[place] = jnp.concatenate(parts + [extra], axis=1).astype(BF16)
        for index in range(2 * COLS):
            target = 2 * ((index // 2) * RINGS + col) + index % 2
            source = outgoing.at[place, index // 2]

            @pl.when(target != me)
            def _():
                rows_to(target, source).start()

            @pl.when(target == me)
            def _():
                pltpu.make_async_copy(source, gathered.at[me], row_recv).start()

    each(8, finish)
    moment_copy = pltpu.make_async_copy(moment_v, moment, local_sem.at[3])
    moment_copy.start()
    stat_copy.wait()
    pltpu.make_async_copy(gathered, gathered, row_recv).wait()

    def tiles(fn, height=TILE, count=SIZE // TILE, start=0):
        def one(t, carry):
            return fn(pl.multiple_of(t * height, height), carry)

        return lax.fori_loop(0, count, one, start)

    def assemble(t, total):
        piece = gathered[pl.ds(t * 8, 8)].astype(F32)
        for c in range(4):
            part = piece[:, c * ROWS:(c + 1) * ROWS].reshape(TILE, LANES)
            block[pl.ds(pl.multiple_of(t * TILE, TILE), TILE), c * LANES:(c + 1) * LANES] = part.astype(BF16)
        return total + jnp.sum(piece[:, 32:40], axis=0)

    adam_sq = lax.fori_loop(0, SIZE // TILE, assemble, jnp.zeros((ROWS, LANES), F32))
    adam_sq = jnp.sum(adam_sq, keepdims=True)

    @pl.when(core == 0)
    def _():
        p_f[...] = lax.dot_general(
            block[...], block[...], (((1,), (1,)), ((), ())), preferred_element_type=F32
        )

    @pl.when(core == 1)
    def _():
        p_f[...] = lax.dot_general(
            block[...], block[...], (((0,), (0,)), ((), ())), preferred_element_type=F32
        )

    def statistic(t, total):
        here = pl.ds(t, TILE)
        value = stat_decay * stat_v[here] + (1.0 - stat_decay) * p_f[here]
        stat_v[here] = value
        square = value * value
        return total + jnp.sum(square.reshape(TILE // ROWS, ROWS, SIZE), axis=0)

    norm = tiles(statistic, start=jnp.zeros((ROWS, SIZE), F32))
    frobenius = jnp.sqrt(jnp.sum(norm, keepdims=True))
    scaling = 5.0 / (2.0 * frobenius)
    first = jnp.sqrt(jnp.sqrt(scaling))

    def halves(value):
        high = value.astype(BF16)
        return high, (value - high.astype(F32)).astype(BF16)

    def put_left(ref, t, value):
        high, low = halves(value)
        here = pl.ds(t, TILE)
        ref[here, 0:SIZE] = high
        ref[here, SIZE:2 * SIZE] = low
        ref[here, 2 * SIZE:3 * SIZE] = high

    def put_right(ref, t, value):
        high, low = halves(value)
        ref[pl.ds(t, TILE)] = high
        ref[pl.ds(SIZE + t, TILE)] = high
        ref[pl.ds(2 * SIZE + t, TILE)] = low

    def product(left, right):
        q_f[...] = jnp.dot(left[...], right[...], preferred_element_type=F32)

    def scaled(t, carry):
        here = pl.ds(t, TILE)
        value = scaling * stat_v[here]
        a_f[here] = value
        put_left(a_l, t, value)
        put_right(t_r, t, value)
        return carry

    def next_moment(m_ref, left, keep):
        product(left, t_r)

        def squared(t, carry):
            here = pl.ds(t, TILE)
            square = q_f[here]
            value = m_ref[here]
            r_f[here] = 1.5625 * value - 0.625 * square
            put_left(b_l, t, 0.0625 * square - 0.625 * value)
            put_right(u_r, t, square)
            return carry

        tiles(squared)
        product(left, u_r)

        def cubed(t, carry):
            here = pl.ds(t, TILE)
            value = r_f[here] + 0.0625 * q_f[here]
            r_f[here] = value
            put_right(t_r, t, value)
            return carry

        tiles(cubed)
        product(b_l, t_r)

        def last(t, carry):
            here = pl.ds(t, TILE)
            value = 1.5625 * r_f[here] + q_f[here]
            put_right(t_r, t, value)
            if keep:
                m_f[here] = value
                put_left(m_l, t, value)
            return carry

        tiles(last)

    def identity(t, scale):
        row = lax.broadcasted_iota(jnp.int32, (TILE, SIZE), 0) + t
        lane = lax.broadcasted_iota(jnp.int32, (TILE, SIZE), 1)
        return jnp.where(row == lane, scale, 0.0)

    def first_iterate(t):
        return identity(t, 1.25) - 0.25 * a_f[pl.ds(t, TILE)]

    tiles(scaled)
    next_moment(a_f, a_l, True)
    product(a_l, t_r)

    def second_iterate(t, carry):
        here = pl.ds(t, TILE)
        value = 1.25 * first_iterate(t) - 0.25 * (1.25 * m_f[here] - 0.25 * q_f[here])
        x_f[here] = value
        put_left(x_l, t, value)
        return carry

    tiles(second_iterate)
    next_moment(m_f, m_l, False)
    product(x_l, t_r)
    count = steps[0]

    def choose(t, carry):
        here = pl.ds(t, TILE)
        third = 1.25 * x_f[here] - 0.25 * q_f[here]
        value = jnp.where(count == 1, first_iterate(t), jnp.where(count == 2, x_f[here], third))
        roots[core, here] = (first * value).astype(BF16)
        return carry

    tiles(choose)

    swap = pltpu.make_async_remote_copy(
        src_ref=roots.at[core],
        dst_ref=roots.at[core],
        send_sem=root_send,
        recv_sem=root_recv,
        device_id={"fsdp": me + 1 - 2 * core},
        device_id_type=MESH,
    )
    arrival = pltpu.make_async_remote_copy(
        src_ref=roots.at[1 - core],
        dst_ref=roots.at[1 - core],
        send_sem=root_send,
        recv_sem=root_recv,
        device_id={"fsdp": me + 1 - 2 * core},
        device_id_type=MESH,
    )
    swap.start()
    arrival.wait_recv()
    middle[...] = jnp.dot(roots[0], block[...], preferred_element_type=F32).astype(BF16)
    q_f[...] = jnp.dot(middle[...], roots[1], preferred_element_type=F32)

    def rounded(t, total):
        here = pl.ds(t, TILE)
        value = q_f[here].astype(BF16).astype(F32)
        direction[here] = value
        square = value * value
        return total + jnp.sum(square.reshape(TILE // ROWS, ROWS, SIZE), axis=0)

    dir_sq = tiles(rounded, start=jnp.zeros((ROWS, SIZE), F32))
    dir_sq = jnp.sum(dir_sq, keepdims=True)
    ratio = jnp.sqrt(adam_sq) / (jnp.sqrt(dir_sq) + ratio_eps)

    def scale(t, carry):
        here = pl.ds(pl.multiple_of(core * (SIZE // 2) + t * TILE, TILE), TILE)
        value = direction[here] * ratio
        parts = [
            value[:, c * LANES:(c + 1) * LANES].reshape(TILE // ROWS, ROWS, LANES) for c in range(4)
        ]
        back[pl.ds(t * 8, 8)] = jnp.concatenate(parts, axis=1).astype(BF16)
        return carry

    lax.fori_loop(0, SIZE // 2 // TILE, scale, 0)

    def back_to(target, source):
        return pltpu.make_async_remote_copy(
            src_ref=source,
            dst_ref=upd.at[chip],
            send_sem=back_send,
            recv_sem=back_recv,
            device_id={"fsdp": target},
            device_id_type=MESH,
        )

    def give(offset):
        slot = lax.rem(lax.rem(me, HALF) + offset, HALF)
        target = core * HALF + slot
        source = back.at[slot]

        @pl.when(target != me)
        def _():
            back_to(target, source).start()

        @pl.when(target == me)
        def _():
            pltpu.make_async_copy(source, upd.at[chip], back_recv).start()

    each(HALF, give)

    def drain(j):
        for way in (0, 1):
            hop1(way, j).wait_send()
            hop2_leaf(way, j).wait_send()
            hop2(way, j).wait_send()
            hop3(way, j).wait_send()
            hop3_leaf(way, j).wait_send()
            hop4(way, j).wait_send()
            hop4(way, j + 4).wait_send()

    each(4, drain)
    swap.wait_send()
    moment_copy.wait()
    sent = gathered.at[pl.ds(0, OWNERS - 1)]
    pltpu.make_async_copy(sent, sent, row_send).wait()
    returns = lax.div(me, HALF) == core

    @pl.when(returns)
    def _():
        sent_back = back.at[pl.ds(0, HALF - 1)]
        pltpu.make_async_copy(sent_back, sent_back, back_send).wait()

    @pl.when(jnp.logical_not(returns))
    def _():
        pltpu.make_async_copy(back, back, back_send).wait()

    pltpu.make_async_copy(back, upd, back_recv).wait()


def on_device(gradients, statistics, newton_steps, second_moment):
    chunk = (COLS, ROWS, SIZE)
    dma = pltpu.SemaphoreType.DMA
    square_f = pltpu.VMEM((SIZE, SIZE), F32)
    square_b = pltpu.VMEM((SIZE, SIZE), BF16)
    left = pltpu.VMEM((SIZE, 3 * SIZE), BF16)
    right = pltpu.VMEM((3 * SIZE, SIZE), BF16)
    anywhere = pl.BlockSpec(memory_space=pl.ANY)
    upd, moment = pl.pallas_call(
        kernel,
        out_shape=(
            jax.ShapeDtypeStruct((HALF, 32, LANES), BF16),
            jax.ShapeDtypeStruct((COLS, RINGS, ROWS, SIZE), F32),
        ),
        in_specs=[anywhere, anywhere, pl.BlockSpec(memory_space=pltpu.SMEM), anywhere],
        out_specs=(anywhere, anywhere),
        scratch_shapes=[
            pltpu.VMEM((WAYS, COLS, RINGS, ROWS, SIZE), BF16),
            square_f,
            pltpu.VMEM((COLS, RINGS, ROWS, SIZE), F32),
            pltpu.VMEM((COLS, RINGS, ROWS, SIZE), F32),
            pltpu.VMEM((2, 4) + chunk, BF16),
            pltpu.VMEM((2, 4) + chunk, BF16),
            pltpu.VMEM((2, 4) + chunk, F32),
            pltpu.VMEM((2, 4) + chunk, F32),
            pltpu.VMEM((2, 4) + chunk, F32),
            pltpu.VMEM((2, 8) + chunk, F32),
            pltpu.VMEM((2, 8) + chunk, F32),
            pltpu.VMEM((RINGS, COLS, MSG, LANES), BF16),
            pltpu.VMEM((OWNERS, MSG, LANES), BF16),
            square_b,
            square_b,
            square_f,
            pltpu.VMEM((HALF, 32, LANES), BF16),
            pltpu.VMEM((2, SIZE, SIZE), BF16),
        ]
        + [square_f] * 6
        + [left] * 4
        + [right] * 2
        + [
            dma((4,)), dma((2, 28)), dma((2, 28)), dma, dma, dma, dma, dma, dma,
        ],
        compiler_params=pltpu.CompilerParams(
            collective_id=0, has_side_effects=True, vmem_limit_bytes=56 * 2**20
        ),
    )(
        gradients.reshape(WAYS, COLS, RINGS, ROWS, SIZE),
        statistics.reshape(SIZE, SIZE),
        newton_steps,
        second_moment.reshape(COLS, RINGS, ROWS, SIZE),
    )
    update = upd.reshape(HALF, 4, ROWS, LANES).transpose(0, 2, 1, 3).reshape(HALF, ROWS, SIZE)
    return update, moment.reshape(HALF, ROWS, SIZE)


def solution(mesh):
    return jax.shard_map(
        on_device,
        mesh=mesh,
        in_specs=(
            P("dp", None, "fsdp", None),
            P(("dp", "fsdp"), None, None),
            P(("dp", "fsdp")),
            P("dp", "fsdp", None),
        ),
        out_specs=(P("dp", "fsdp", None), P("dp", "fsdp", None)),
        check_vma=False,
    )
```

```python
import jax
import jax.numpy as jnp
from jax import lax
from jax.experimental import pallas as pl
from jax.experimental.pallas import tpu as pltpu
from jax.sharding import PartitionSpec as P

stat_decay = 0.9
moment_decay = 0.95
adam_eps = 1e-08
ratio_eps = 1e-06
MESH = pl.DeviceIdType.MESH
F32 = jnp.float32
BF16 = jnp.bfloat16
LANES = 128
ROWS = 8
TILE = 64
SIZE = 512
WAYS = 8
COLS = 4
RINGS = 8
OWNERS = 64
HALF = OWNERS // 2
PART = 256


def kernel(
    grad, stats, steps, second, upd, moment,
    own, stat_v, second_v, moment_v,
    r1, leaf, r2, s2, s3, r3, r4,
    outgoing, gathered, sums_out, sums_in, block, middle, back, roots,
    a_f, p_f, q_f, m_f, n_f,
    a_l, b_l, m_l, n_l, u_l, ra, rb, rc,
    local_sem, ring_send, ring_recv, row_send, row_recv, pair_send, pair_recv,
    sum_send, sum_recv, root_send, root_recv, back_send, back_recv,
):
    y = lax.axis_index("dp")
    me = lax.axis_index("fsdp")
    core = lax.rem(me, 2)
    chip = lax.div(me, 2)
    x = lax.div(chip, RINGS)
    z = lax.rem(chip, RINGS)
    partner = me + 1 - 2 * core

    def each(count, fn, first=0):
        def one(j, carry):
            fn(j)
            return carry

        lax.fori_loop(first, count, one, 0)

    barrier = pltpu.get_barrier_semaphore()
    for shift in (1, WAYS - 1):
        pl.semaphore_signal(
            barrier, inc=1, device_id={"dp": lax.rem(y + shift, WAYS)}, device_id_type=MESH
        )

    def greet(t):
        offset = lax.rem(t, COLS) * 2 * RINGS + lax.div(t, COLS)
        pl.semaphore_signal(
            barrier, inc=1, device_id={"fsdp": lax.rem(me + offset, OWNERS)}, device_id_type=MESH
        )

    each(OWNERS, greet, 1)
    own_copy = pltpu.make_async_copy(grad, own, local_sem.at[0])
    stat_copy = pltpu.make_async_copy(stats, stat_v, local_sem.at[1])
    second_copy = pltpu.make_async_copy(second, second_v, local_sem.at[2])
    own_copy.start()
    second_copy.start()
    stat_copy.start()
    pl.semaphore_wait(barrier, OWNERS + 1)

    def group(way, distance):
        return lax.rem(y + (distance if way == 0 else WAYS - distance), WAYS)

    def shift_of(place):
        half = lax.div(place + 1, 2)
        return 4 + half * (1 - 2 * lax.rem(place, 2))

    def column(place):
        return lax.rem(z + shift_of(place), RINGS)

    def ring(way, index, source, target):
        return pltpu.make_async_remote_copy(
            src_ref=source,
            dst_ref=target,
            send_sem=ring_send.at[way],
            recv_sem=ring_recv.at[way, index],
            device_id={"dp": group(way, 1)},
            device_id_type=MESH,
        )

    def mine(way, distance, place):
        return own[group(way, distance), :, column(place)].astype(F32)

    def hop1(way, j):
        place = j + 4 * way
        return ring(way, j, grad.at[group(way, 4), :, column(place)], r1.at[way, j])

    def hop2_leaf(way, j):
        place = j + 4 * (1 - way)
        return ring(way, 4 + j, grad.at[group(way, 3), :, column(place)], leaf.at[way, j])

    def hop2(way, j):
        return ring(way, 8 + j, s2.at[way, j], r2.at[way, j])

    def hop3(way, j):
        return ring(way, 12 + j, r2.at[way, j], r3.at[way, j + 4 * way])

    def hop3_leaf(way, j):
        return ring(way, 16 + j, s3.at[way, j], r3.at[way, j + 4 * (1 - way)])

    def hop4(way, place):
        return ring(way, 20 + place, r3.at[way, place], r4.at[way, place])

    def start1(j):
        hop1(0, j).start()
        hop1(1, j).start()

    def start2_leaf(j):
        hop2_leaf(0, j).start()
        hop2_leaf(1, j).start()

    each(4, start1)
    each(4, start2_leaf)
    own_copy.wait()

    def start2(j):
        for way in (0, 1):
            hop1(way, j).wait_recv()
            s2[way, j] = r1[way, j].astype(F32) + mine(way, 3, j + 4 * way)
            hop2(way, j).start()

    each(4, start2)

    def long3(way, j):
        hop2(way, j).wait_recv()
        r2[way, j] = r2[way, j] + mine(way, 2, j + 4 * way)
        hop3(way, j).start()

    def short3(way, j):
        hop2_leaf(way, j).wait_recv()
        s3[way, j] = leaf[way, j].astype(F32) + mine(way, 2, j + 4 * (1 - way))
        hop3_leaf(way, j).start()

    def start3_low(j):
        short3(1, j)
        long3(0, j)

    def start3_high(j):
        short3(0, j)
        long3(1, j)

    each(4, start3_low)
    each(4, start3_high)

    def step4(way, place, arrival):
        arrival.wait_recv()
        r3[way, place] = r3[way, place] + mine(way, 1, place)
        hop4(way, place).start()

    def start4_low(j):
        step4(0, j, hop3(0, j))
        step4(1, j, hop3_leaf(1, j))

    def start4_high(j):
        step4(0, j + 4, hop3_leaf(0, j))
        step4(1, j + 4, hop3(1, j))

    each(4, start4_low)
    each(4, start4_high)
    second_copy.wait()

    def finish(place):
        hop4(0, place).wait_recv()
        hop4(1, place).wait_recv()
        col = column(place)
        total = r4[0, place] + r4[1, place] + own[y, :, col].astype(F32)
        mean = total * (1.0 / WAYS)
        new = moment_decay * second_v[:, col] + (1.0 - moment_decay) * mean * mean
        moment_v[:, col] = new
        adam = mean / (jnp.sqrt(new) + adam_eps)
        square = adam * adam
        parts = [mean[:, :, c * LANES:(c + 1) * LANES] for c in range(4)]
        squares = [square[:, :, c * LANES:(c + 1) * LANES] for c in range(4)]
        outgoing[place] = jnp.concatenate(parts, axis=1).astype(BF16)
        for index in range(COLS):
            target = 2 * (index * RINGS + col) + core
            source = outgoing.at[place, index]

            @pl.when(target != me)
            def _():
                pltpu.make_async_remote_copy(
                    src_ref=source,
                    dst_ref=gathered.at[core, place, x],
                    send_sem=row_send,
                    recv_sem=row_recv.at[place],
                    device_id={"fsdp": target},
                    device_id_type=MESH,
                ).start()

            @pl.when(target == me)
            def _():
                pltpu.make_async_copy(source, gathered.at[core, place, x], row_recv.at[place]).start()

        sums_out[place] = jnp.sum(
            (squares[0] + squares[1]) + (squares[2] + squares[3]), axis=1, keepdims=True
        )
        for index in range(2 * COLS):
            target = 2 * ((index // 2) * RINGS + col) + index % 2
            source = sums_out.at[place, index // 2]

            @pl.when(target != me)
            def _():
                pltpu.make_async_remote_copy(
                    src_ref=source,
                    dst_ref=sums_in.at[me],
                    send_sem=sum_send,
                    recv_sem=sum_recv,
                    device_id={"fsdp": target},
                    device_id_type=MESH,
                ).start()

            @pl.when(target == me)
            def _():
                pltpu.make_async_copy(source, sums_in.at[me], sum_recv).start()

    each(8, finish)
    moment_copy = pltpu.make_async_copy(moment_v, moment, local_sem.at[3])
    moment_copy.start()

    def to_partner(source, target, send, recv):
        return pltpu.make_async_remote_copy(
            src_ref=source,
            dst_ref=target,
            send_sem=send,
            recv_sem=recv,
            device_id={"fsdp": partner},
            device_id_type=MESH,
        )

    def forward(place):
        here = gathered.at[core, place]
        pltpu.make_async_copy(here, here, row_recv.at[place]).wait()
        to_partner(here, here, pair_send, pair_recv).start()

    each(8, forward)
    stat_copy.wait()
    there = gathered.at[1 - core]
    pltpu.make_async_copy(there, there, pair_recv).wait()

    def assemble(place):
        source_z = lax.rem(z + RINGS - shift_of(place) + RINGS, RINGS)
        for index in range(COLS):
            pair = [gathered[c, place, index].astype(F32) for c in (0, 1)]
            start = pl.multiple_of((index * RINGS + source_z) * 16, 16)
            for c in range(4):
                both = [p[c * ROWS:(c + 1) * ROWS] for p in pair]
                block[pl.ds(start, 16), c * LANES:(c + 1) * LANES] = jnp.concatenate(both, axis=0).astype(BF16)

    each(8, assemble)

    @pl.when(core == 0)
    def _():
        p_f[...] = lax.dot_general(
            block[...], block[...], (((1,), (1,)), ((), ())), preferred_element_type=F32
        )

    @pl.when(core == 1)
    def _():
        p_f[...] = lax.dot_general(
            block[...], block[...], (((0,), (0,)), ((), ())), preferred_element_type=F32
        )

    def square_sum(value):
        return jnp.sum((value * value).reshape(value.shape[0] // ROWS, ROWS, SIZE), axis=0)

    norm = jnp.zeros((ROWS, SIZE), F32)
    for t in range(0, SIZE, TILE):
        here = slice(t, t + TILE)
        value = stat_decay * stat_v[here] + (1.0 - stat_decay) * p_f[here]
        stat_v[here] = value
        norm = norm + square_sum(value)
    frobenius = jnp.sqrt(jnp.sum(norm, keepdims=True))
    scaling = 5.0 / (2.0 * frobenius)
    first = jnp.sqrt(jnp.sqrt(scaling))

    def halves(value):
        high = value.astype(BF16)
        return high, (value - high.astype(F32)).astype(BF16)

    def put_left(ref, t, parts):
        high, low = parts
        here = slice(t, t + TILE)
        ref[here, 0:SIZE] = high
        ref[here, SIZE:2 * SIZE] = low
        ref[here, 2 * SIZE:3 * SIZE] = high

    def put_right(ref, t, parts):
        high, low = parts
        ref[t:t + TILE] = high
        ref[SIZE + t:SIZE + t + TILE] = high
        ref[2 * SIZE + t:2 * SIZE + t + TILE] = low

    def product(left, right, use):
        for h in range(0, SIZE, PART):
            q_f[h:h + PART] = jnp.dot(left[h:h + PART], right[...], preferred_element_type=F32)
            for t in range(h, h + PART, TILE):
                use(t, slice(t, t + TILE), q_f[t:t + TILE])

    def identity(t, scale):
        row = lax.broadcasted_iota(jnp.int32, (TILE, SIZE), 0) + t
        lane = lax.broadcasted_iota(jnp.int32, (TILE, SIZE), 1)
        return jnp.where(row == lane, scale, 0.0)

    for t in range(0, SIZE, TILE):
        here = slice(t, t + TILE)
        value = scaling * stat_v[here]
        a_f[here] = value
        parts = halves(value)
        put_left(a_l, t, parts)
        put_right(ra, t, parts)

    def squared(t, here, q):
        p_f[here] = q
        put_left(b_l, t, halves(0.0625 * q - 0.625 * a_f[here]))
        put_right(rb, t, halves(q))

    def cubed(t, here, q):
        value = 1.5625 * a_f[here] - 0.625 * p_f[here] + 0.0625 * q
        n_f[here] = value
        put_right(rc, t, halves(value))

    def moved(t, here, q):
        value = 1.5625 * n_f[here] + q
        m_f[here] = value
        parts = halves(value)
        put_left(m_l, t, parts)
        put_right(ra, t, parts)

    def squared_again(t, here, q):
        m = m_f[here]
        value = 1.25 * m - 0.25 * q
        n_f[here] = value
        put_left(n_l, t, halves(value))
        put_right(rb, t, halves(0.0625 * q - 0.625 * m))

    def fourth(t, here, q):
        value = 1.5625 * n_f[here] + q
        p_f[here] = value
        put_left(u_l, t, halves(value))

    count = steps[0]

    def last_factor(t, here, q):
        second_w = identity(t, 1.25) - 0.25 * m_f[here]
        third = 1.25 * second_w - 0.25 * (1.5625 * p_f[here] + q)
        value = jnp.where(count == 2, second_w, third)
        n_f[here] = value
        put_right(rc, t, halves(value))

    def swap_half(h):
        here = roots.at[core, pl.ds(h * PART, PART)]
        return to_partner(here, here, root_send.at[h], root_recv.at[h])

    def swapped_half(h):
        here = roots.at[1 - core, pl.ds(h * PART, PART)]
        return to_partner(here, here, root_send.at[h], root_recv.at[h])

    def choose(t, here, q):
        one = identity(t, 1.25) - 0.25 * a_f[here]
        more = 1.25 * n_f[here] - 0.25 * q
        value = jnp.where(count == 1, one, more)
        roots[core, here] = (first * value).astype(BF16)
        if (t + TILE) % PART == 0:
            swap_half(t // PART).start()

    product(a_l, ra, squared)
    product(a_l, rb, cubed)
    product(b_l, rc, moved)
    product(m_l, ra, squared_again)
    product(n_l, rb, fourth)
    product(u_l, rb, last_factor)
    product(a_l, rc, choose)

    adam_sums = sums_in.at[...]
    pltpu.make_async_copy(adam_sums, adam_sums, sum_recv).wait()
    adam_sq = jnp.sum(jnp.sum(sums_in[...], axis=0), keepdims=True)
    for h in (0, 1):
        @pl.when(core == 1)
        def _():
            swapped_half(h).wait_recv()

        here = slice(h * PART, (h + 1) * PART)
        middle[here] = jnp.dot(roots[0, here], block[...], preferred_element_type=F32).astype(BF16)

    @pl.when(core == 0)
    def _():
        swapped_half(0).wait_recv()
        swapped_half(1).wait_recv()

    dir_sq = jnp.zeros((ROWS, SIZE), F32)
    for h in range(0, SIZE, PART):
        q_f[h:h + PART] = jnp.dot(middle[h:h + PART], roots[1], preferred_element_type=F32)
        for t in range(h, h + PART, TILE):
            here = slice(t, t + TILE)
            value = q_f[here].astype(BF16).astype(F32)
            q_f[here] = value
            dir_sq = dir_sq + square_sum(value)
    dir_sq = jnp.sum(dir_sq, keepdims=True)
    ratio = jnp.sqrt(adam_sq) / (jnp.sqrt(dir_sq) + ratio_eps)

    def scale(t):
        here = pl.ds(pl.multiple_of(core * PART + t * TILE, TILE), TILE)
        value = q_f[here] * ratio
        parts = [
            value[:, c * LANES:(c + 1) * LANES].reshape(TILE // ROWS, ROWS, LANES) for c in range(4)
        ]
        back[pl.ds(t * 8, 8)] = jnp.concatenate(parts, axis=1).astype(BF16)
        for index in range(8):
            slot = t * 8 + index
            target = core * HALF + slot
            source = back.at[slot]

            @pl.when(target != me)
            def _():
                pltpu.make_async_remote_copy(
                    src_ref=source,
                    dst_ref=upd.at[chip],
                    send_sem=back_send,
                    recv_sem=back_recv,
                    device_id={"fsdp": target},
                    device_id_type=MESH,
                ).start()

            @pl.when(target == me)
            def _():
                pltpu.make_async_copy(source, upd.at[chip], back_recv).start()

    each(PART // TILE, scale)

    for way in (0, 1):
        sent = own.at[pl.ds(0, 6)]
        pltpu.make_async_copy(sent, sent, ring_send.at[way]).wait()
    swap_half(0).wait_send()
    swap_half(1).wait_send()
    here = gathered.at[core]
    pltpu.make_async_copy(here, here, pair_send).wait()
    sent = back.at[pl.ds(0, HALF - 1)]
    pltpu.make_async_copy(sent, sent, row_send).wait()
    sent_sums = sums_in.at[pl.ds(0, OWNERS - 1)]
    pltpu.make_async_copy(sent_sums, sent_sums, sum_send).wait()
    moment_copy.wait()
    returns = lax.div(me, HALF) == core

    @pl.when(returns)
    def _():
        sent_back = back.at[pl.ds(0, HALF - 1)]
        pltpu.make_async_copy(sent_back, sent_back, back_send).wait()

    @pl.when(jnp.logical_not(returns))
    def _():
        pltpu.make_async_copy(back, back, back_send).wait()

    pltpu.make_async_copy(back, upd, back_recv).wait()


def write_out(upd, moment_in, update, moment, upd_v, update_v, moment_v, sems):
    rows_in = pltpu.make_async_copy(upd, upd_v, sems.at[0])
    moment_here = pltpu.make_async_copy(moment_in, moment_v, sems.at[1])
    rows_in.start()
    moment_here.start()
    moment_here.wait()
    moment_out = pltpu.make_async_copy(moment_v, moment, sems.at[2])
    moment_out.start()
    rows_in.wait()
    wide = upd_v[...].astype(F32)
    for c in range(4):
        update_v[:, :, c * LANES:(c + 1) * LANES] = wide[:, c * ROWS:(c + 1) * ROWS].astype(BF16)
    rows_out = pltpu.make_async_copy(update_v, update, sems.at[3])
    rows_out.start()
    moment_out.wait()
    rows_out.wait()


def on_device(gradients, statistics, newton_steps, second_moment):
    chunk = (COLS, ROWS, SIZE)
    dma = pltpu.SemaphoreType.DMA
    square_f = pltpu.VMEM((SIZE, SIZE), F32)
    square_b = pltpu.VMEM((SIZE, SIZE), BF16)
    left = pltpu.VMEM((SIZE, 3 * SIZE), BF16)
    right = pltpu.VMEM((3 * SIZE, SIZE), BF16)
    anywhere = pl.BlockSpec(memory_space=pl.ANY)
    group_f = pltpu.VMEM((COLS, RINGS, ROWS, SIZE), F32)
    upd, moment = pl.pallas_call(
        kernel,
        out_shape=(
            jax.ShapeDtypeStruct((HALF, 32, LANES), BF16),
            jax.ShapeDtypeStruct((COLS, RINGS, ROWS, SIZE), F32),
        ),
        in_specs=[anywhere, anywhere, pl.BlockSpec(memory_space=pltpu.SMEM), anywhere],
        out_specs=(anywhere, anywhere),
        scratch_shapes=[
            pltpu.VMEM((WAYS, COLS, RINGS, ROWS, SIZE), BF16),
            square_f,
            group_f,
            group_f,
            pltpu.VMEM((2, 4) + chunk, BF16),
            pltpu.VMEM((2, 4) + chunk, BF16),
            pltpu.VMEM((2, 4) + chunk, F32),
            pltpu.VMEM((2, 4) + chunk, F32),
            pltpu.VMEM((2, 4) + chunk, F32),
            pltpu.VMEM((2, 8) + chunk, F32),
            pltpu.VMEM((2, 8) + chunk, F32),
            pltpu.VMEM((RINGS, COLS, 32, LANES), BF16),
            pltpu.VMEM((2, RINGS, COLS, 32, LANES), BF16),
            pltpu.VMEM((RINGS, COLS, 1, LANES), F32),
            pltpu.VMEM((OWNERS, 1, LANES), F32),
            square_b,
            square_b,
            pltpu.VMEM((HALF, 32, LANES), BF16),
            pltpu.VMEM((2, SIZE, SIZE), BF16),
        ]
        + [square_f] * 5
        + [left] * 5
        + [right] * 3
        + [
            dma((4,)), dma((2,)), dma((2, 28)), dma, dma((8,)), dma, dma,
            dma, dma, dma((2,)), dma((2,)), dma, dma,
        ],
        compiler_params=pltpu.CompilerParams(
            collective_id=0, has_side_effects=True, vmem_limit_bytes=56 * 2**20
        ),
    )(
        gradients.reshape(WAYS, COLS, RINGS, ROWS, SIZE),
        statistics.reshape(SIZE, SIZE),
        newton_steps,
        second_moment.reshape(COLS, RINGS, ROWS, SIZE),
    )
    return pl.pallas_call(
        write_out,
        out_shape=(
            jax.ShapeDtypeStruct((HALF, ROWS, SIZE), BF16),
            jax.ShapeDtypeStruct((HALF, ROWS, SIZE), F32),
        ),
        in_specs=[anywhere, anywhere],
        out_specs=(anywhere, anywhere),
        scratch_shapes=[
            pltpu.VMEM((HALF, 32, LANES), BF16),
            pltpu.VMEM((HALF, ROWS, SIZE), BF16),
            pltpu.VMEM((HALF, ROWS, SIZE), F32),
            dma((4,)),
        ],
    )(upd, moment.reshape(HALF, ROWS, SIZE))


def solution(mesh):
    return jax.shard_map(
        on_device,
        mesh=mesh,
        in_specs=(
            P("dp", None, "fsdp", None),
            P(("dp", "fsdp"), None, None),
            P(("dp", "fsdp")),
            P("dp", "fsdp", None),
        ),
        out_specs=(P("dp", "fsdp", None), P("dp", "fsdp", None)),
        check_vma=False,
    )
```

```python
import jax
import jax.numpy as jnp
from jax import lax
from jax.experimental import pallas as pl
from jax.experimental.pallas import tpu as pltpu
from jax.sharding import PartitionSpec as P

stat_decay = 0.9
moment_decay = 0.95
adam_eps = 1e-08
ratio_eps = 1e-06
MESH = pl.DeviceIdType.MESH
F32 = jnp.float32
BF16 = jnp.bfloat16
LANES = 128
ROWS = 8
TILE = 64
SIZE = 512
WAYS = 8
COLS = 4
RINGS = 8
OWNERS = 64
HALF = OWNERS // 2
PART = 256


def kernel(
    grad, stats, steps, second, upd, moment,
    own, stat_v, second_v, moment_v,
    r1, leaf, codes_out, codes_in, units_out, units_in, steps_v,
    outgoing, gathered, sums_out, sums_in, block, middle, back, roots,
    a_f, p_f, q_f, m_f, n_f,
    a_l, b_l, m_l, n_l, u_l, ra, rb, rc,
    local_sem, raw_send, raw_recv, code_send, code_recv, unit_send, unit_recv, row_send, row_recv, pair_send, pair_recv,
    sum_send, sum_recv, root_send, root_recv, back_send, back_recv,
):
    y = lax.axis_index("dp")
    me = lax.axis_index("fsdp")
    core = lax.rem(me, 2)
    chip = lax.div(me, 2)
    x = lax.div(chip, RINGS)
    z = lax.rem(chip, RINGS)
    partner = me + 1 - 2 * core

    def each(count, fn, first=0):
        def one(j, carry):
            fn(j)
            return carry

        lax.fori_loop(first, count, one, 0)

    barrier = pltpu.get_barrier_semaphore()
    for shift in (1, WAYS - 1):
        pl.semaphore_signal(
            barrier, inc=1, device_id={"dp": lax.rem(y + shift, WAYS)}, device_id_type=MESH
        )

    def greet(t):
        offset = lax.rem(t, COLS) * 2 * RINGS + lax.div(t, COLS)
        pl.semaphore_signal(
            barrier, inc=1, device_id={"fsdp": lax.rem(me + offset, OWNERS)}, device_id_type=MESH
        )

    each(OWNERS, greet, 1)
    own_copy = pltpu.make_async_copy(grad, own, local_sem.at[0])
    stat_copy = pltpu.make_async_copy(stats, stat_v, local_sem.at[1])
    second_copy = pltpu.make_async_copy(second, second_v, local_sem.at[2])
    steps_copy = pltpu.make_async_copy(steps, steps_v, local_sem.at[4])
    own_copy.start()
    second_copy.start()
    stat_copy.start()
    steps_copy.start()
    pl.semaphore_wait(barrier, OWNERS + 1)

    def group(way, distance):
        return lax.rem(y + (distance if way == 0 else WAYS - distance), WAYS)

    def shift_of(place):
        half = lax.div(place + 1, 2)
        return 4 + half * (1 - 2 * lax.rem(place, 2))

    def column(place):
        return lax.rem(z + shift_of(place), RINGS)

    def ring(way, source, target, send, recv):
        return pltpu.make_async_remote_copy(
            src_ref=source,
            dst_ref=target,
            send_sem=send,
            recv_sem=recv,
            device_id={"dp": group(way, 1)},
            device_id_type=MESH,
        )

    def raw(way, index, distance, place, target):
        source = grad.at[group(way, distance), :, column(place)]
        return ring(way, source, target, raw_send.at[way], raw_recv.at[way, index])

    def hop1(way, j):
        return raw(way, j, 4, j + 4 * way, r1.at[way, j])

    def hop2_leaf(way, j):
        return raw(way, 4 + j, 3, j + 4 * (1 - way), leaf.at[way, j])

    def codes(way, index):
        return ring(
            way, codes_out.at[way, index], codes_in.at[way, index], code_send.at[way], code_recv.at[way, index]
        )

    def units(way, index):
        return ring(
            way, units_out.at[way, index], units_in.at[way, index], unit_send.at[way], unit_recv.at[way, index]
        )

    def near_power(value):
        wide = value * (2.0**23 + 1.0)
        return wide - (wide - value)

    def columns_of(value):
        return [value[:, :, c * LANES:(c + 1) * LANES] for c in range(4)]

    def send_sum(way, index, value):
        parts = columns_of(value)
        size = [jnp.abs(part) for part in parts]
        largest = jnp.maximum(jnp.maximum(size[0], size[1]), jnp.maximum(size[2], size[3]))
        largest = jnp.maximum(jnp.max(largest, axis=1, keepdims=True), 1e-25)
        power = near_power(largest)
        units_out[way, index] = power * 2.0**-14
        units(way, index).start()
        inverse = near_power(2.0**14 / power)
        near = [(part * inverse + 1.5 * 2.0**23) - 1.5 * 2.0**23 for part in parts]
        codes_out[way, index] = jnp.concatenate(near, axis=2).astype(jnp.int32).astype(jnp.int16)
        codes(way, index).start()

    def received(way, index):
        units(way, index).wait_recv()
        codes(way, index).wait_recv()
        unit = units_in[way, index]
        parts = columns_of(codes_in[way, index].astype(jnp.int32).astype(F32))
        return jnp.concatenate([part * unit for part in parts], axis=2)

    def mine(way, distance, place):
        return own[group(way, distance), :, column(place)].astype(F32)

    def start1(j):
        hop1(0, j).start()
        hop1(1, j).start()

    def start2_leaf(j):
        hop2_leaf(0, j).start()
        hop2_leaf(1, j).start()

    each(4, start1)
    each(4, start2_leaf)
    own_copy.wait()

    def start2(j):
        for way in (0, 1):
            hop1(way, j).wait_recv()
            send_sum(way, j, r1[way, j].astype(F32) + mine(way, 3, j + 4 * way))

    each(4, start2)

    def long3(way, j):
        place = j + 4 * way
        send_sum(way, 4 + place, received(way, j) + mine(way, 2, place))

    def short3(way, j):
        place = j + 4 * (1 - way)
        hop2_leaf(way, j).wait_recv()
        send_sum(way, 4 + place, leaf[way, j].astype(F32) + mine(way, 2, place))

    def start3_low(j):
        short3(1, j)
        long3(0, j)

    def start3_high(j):
        short3(0, j)
        long3(1, j)

    each(4, start3_low)
    each(4, start3_high)

    def start4(place):
        for way in (0, 1):
            send_sum(way, 12 + place, received(way, 4 + place) + mine(way, 1, place))

    each(8, start4)
    second_copy.wait()

    def finish(place):
        col = column(place)
        total = received(0, 12 + place) + received(1, 12 + place) + own[y, :, col].astype(F32)
        mean = total * (1.0 / WAYS)
        new = moment_decay * second_v[:, col] + (1.0 - moment_decay) * mean * mean
        moment_v[:, col] = new
        adam = mean / (jnp.sqrt(new) + adam_eps)
        square = adam * adam
        squares = columns_of(square)
        outgoing[place] = jnp.concatenate(columns_of(mean), axis=1).astype(BF16)
        for index in range(COLS):
            target = 2 * (index * RINGS + col) + core
            source = outgoing.at[place, index]

            @pl.when(target != me)
            def _():
                pltpu.make_async_remote_copy(
                    src_ref=source,
                    dst_ref=gathered.at[core, place, x],
                    send_sem=row_send,
                    recv_sem=row_recv.at[place],
                    device_id={"fsdp": target},
                    device_id_type=MESH,
                ).start()

            @pl.when(target == me)
            def _():
                pltpu.make_async_copy(source, gathered.at[core, place, x], row_recv.at[place]).start()

        sums_out[place] = jnp.sum(
            (squares[0] + squares[1]) + (squares[2] + squares[3]), axis=1, keepdims=True
        )
        for index in range(2 * COLS):
            target = 2 * ((index // 2) * RINGS + col) + index % 2
            source = sums_out.at[place, index // 2]

            @pl.when(target != me)
            def _():
                pltpu.make_async_remote_copy(
                    src_ref=source,
                    dst_ref=sums_in.at[me],
                    send_sem=sum_send,
                    recv_sem=sum_recv,
                    device_id={"fsdp": target},
                    device_id_type=MESH,
                ).start()

            @pl.when(target == me)
            def _():
                pltpu.make_async_copy(source, sums_in.at[me], sum_recv).start()

    each(8, finish)
    moment_copy = pltpu.make_async_copy(moment_v, moment, local_sem.at[3])
    moment_copy.start()

    def to_partner(source, target, send, recv):
        return pltpu.make_async_remote_copy(
            src_ref=source,
            dst_ref=target,
            send_sem=send,
            recv_sem=recv,
            device_id={"fsdp": partner},
            device_id_type=MESH,
        )

    def forward(place):
        here = gathered.at[core, place]
        pltpu.make_async_copy(here, here, row_recv.at[place]).wait()
        to_partner(here, here, pair_send, pair_recv).start()

    each(8, forward)
    stat_copy.wait()
    there = gathered.at[1 - core]
    pltpu.make_async_copy(there, there, pair_recv).wait()

    def assemble(place):
        source_z = lax.rem(z + RINGS - shift_of(place) + RINGS, RINGS)
        for index in range(COLS):
            pair = [gathered[c, place, index].astype(F32) for c in (0, 1)]
            start = pl.multiple_of((index * RINGS + source_z) * 16, 16)
            for c in range(4):
                both = [p[c * ROWS:(c + 1) * ROWS] for p in pair]
                block[pl.ds(start, 16), c * LANES:(c + 1) * LANES] = jnp.concatenate(both, axis=0).astype(BF16)

    each(8, assemble)

    @pl.when(core == 0)
    def _():
        p_f[...] = lax.dot_general(
            block[...], block[...], (((1,), (1,)), ((), ())), preferred_element_type=F32
        )

    @pl.when(core == 1)
    def _():
        p_f[...] = lax.dot_general(
            block[...], block[...], (((0,), (0,)), ((), ())), preferred_element_type=F32
        )

    def square_sum(value):
        return jnp.sum((value * value).reshape(value.shape[0] // ROWS, ROWS, value.shape[1]), axis=0)

    norm = jnp.zeros((ROWS, SIZE), F32)
    for t in range(0, SIZE, TILE):
        here = slice(t, t + TILE)
        value = stat_decay * stat_v[here] + (1.0 - stat_decay) * p_f[here]
        stat_v[here] = value
        norm = norm + square_sum(value)
    frobenius = jnp.sqrt(jnp.sum(norm, keepdims=True))
    scaling = 5.0 / (2.0 * frobenius)
    first = jnp.sqrt(jnp.sqrt(scaling))

    def halves(value):
        high = value.astype(BF16)
        return high, (value - high.astype(F32)).astype(BF16)

    def put_left(ref, t, cols, parts):
        high, low = parts
        here = slice(t, t + TILE)
        for shift, part in ((0, high), (SIZE, low), (2 * SIZE, high)):
            ref[here, cols.start + shift:cols.stop + shift] = part

    def put_right(ref, t, cols, parts):
        high, low = parts
        for shift, part in ((0, high), (SIZE, high), (2 * SIZE, low)):
            ref[t + shift:t + shift + TILE, cols] = part

    def product(left, right, use):
        for h in range(0, SIZE, PART):
            cols = slice(h, h + PART)
            q_f[:, cols] = jnp.dot(left[...], right[:, cols], preferred_element_type=F32)
            for t in range(0, SIZE, TILE):
                here = (slice(t, t + TILE), cols)
                use(t, cols, here, q_f[here])

    def identity(t, cols, scale):
        shape = (TILE, cols.stop - cols.start)
        row = lax.broadcasted_iota(jnp.int32, shape, 0) + t
        lane = lax.broadcasted_iota(jnp.int32, shape, 1) + cols.start
        return jnp.where(row == lane, scale, 0.0)

    everything = slice(0, SIZE)
    for t in range(0, SIZE, TILE):
        here = slice(t, t + TILE)
        value = scaling * stat_v[here]
        a_f[here] = value
        parts = halves(value)
        put_left(a_l, t, everything, parts)
        put_right(ra, t, everything, parts)

    def squared(t, cols, here, q):
        p_f[here] = q
        put_left(b_l, t, cols, halves(0.0625 * q - 0.625 * a_f[here]))
        put_right(rb, t, cols, halves(q))

    def cubed(t, cols, here, q):
        value = 1.5625 * a_f[here] - 0.625 * p_f[here] + 0.0625 * q
        n_f[here] = value
        put_right(rc, t, cols, halves(value))

    def moved(t, cols, here, q):
        value = 1.5625 * n_f[here] + q
        m_f[here] = value
        parts = halves(value)
        put_left(m_l, t, cols, parts)
        put_right(ra, t, cols, parts)

    def squared_again(t, cols, here, q):
        m = m_f[here]
        value = 1.25 * m - 0.25 * q
        n_f[here] = value
        put_left(n_l, t, cols, halves(value))
        put_right(rb, t, cols, halves(0.0625 * q - 0.625 * m))

    def fourth(t, cols, here, q):
        value = 1.5625 * n_f[here] + q
        p_f[here] = value
        put_left(u_l, t, cols, halves(value))

    steps_copy.wait()
    count = steps_v[0]

    def last_factor(t, cols, here, q):
        second_w = identity(t, cols, 1.25) - 0.25 * m_f[here]
        third = 1.25 * second_w - 0.25 * (1.5625 * p_f[here] + q)
        value = jnp.where(count == 2, second_w, third)
        n_f[here] = value
        put_right(rc, t, cols, halves(value))

    def swap_half(h):
        here = roots.at[core, h]
        return to_partner(here, here, root_send.at[h], root_recv.at[h])

    def swapped_half(h):
        here = roots.at[1 - core, h]
        return to_partner(here, here, root_send.at[h], root_recv.at[h])

    def choose(t, cols, here, q):
        one = identity(t, cols, 1.25) - 0.25 * a_f[here]
        more = 1.25 * n_f[here] - 0.25 * q
        value = jnp.where(count == 1, one, more)
        h = cols.start // PART
        roots[core, h, t:t + TILE] = (first * value).astype(BF16)
        if t + TILE == SIZE:
            swap_half(h).start()

    product(a_l, ra, squared)
    product(a_l, rb, cubed)
    product(b_l, rc, moved)
    product(m_l, ra, squared_again)
    product(n_l, rb, fourth)
    product(u_l, rb, last_factor)
    product(a_l, rc, choose)

    adam_sums = sums_in.at[...]
    pltpu.make_async_copy(adam_sums, adam_sums, sum_recv).wait()
    adam_sq = jnp.sum(jnp.sum(sums_in[...], axis=0), keepdims=True)
    @pl.when(core == 1)
    def _():
        swapped_half(0).wait_recv()
        swapped_half(1).wait_recv()

    total = jnp.dot(roots[0, 0], block[0:PART], preferred_element_type=F32)
    total = total + jnp.dot(roots[0, 1], block[PART:SIZE], preferred_element_type=F32)
    middle[...] = total.astype(BF16)

    dir_sq = jnp.zeros((ROWS, PART), F32)
    for h in (0, 1):
        @pl.when(core == 0)
        def _():
            swapped_half(h).wait_recv()

        cols = slice(h * PART, (h + 1) * PART)
        q_f[:, cols] = jnp.dot(middle[...], roots[1, h], preferred_element_type=F32)
        for t in range(0, SIZE, TILE):
            here = slice(t, t + TILE)
            value = q_f[here, cols].astype(BF16).astype(F32)
            q_f[here, cols] = value
            dir_sq = dir_sq + square_sum(value)
    dir_sq = jnp.sum(dir_sq, keepdims=True)
    ratio = jnp.sqrt(adam_sq) / (jnp.sqrt(dir_sq) + ratio_eps)

    def scale(t):
        here = pl.ds(pl.multiple_of(core * PART + t * TILE, TILE), TILE)
        value = q_f[here] * ratio
        parts = [
            value[:, c * LANES:(c + 1) * LANES].reshape(TILE // ROWS, ROWS, LANES) for c in range(4)
        ]
        back[pl.ds(t * 8, 8)] = jnp.concatenate(parts, axis=1).astype(BF16)
        for index in range(8):
            slot = t * 8 + index
            target = core * HALF + slot
            source = back.at[slot]

            @pl.when(target != me)
            def _():
                pltpu.make_async_remote_copy(
                    src_ref=source,
                    dst_ref=upd.at[chip],
                    send_sem=back_send,
                    recv_sem=back_recv,
                    device_id={"fsdp": target},
                    device_id_type=MESH,
                ).start()

            @pl.when(target == me)
            def _():
                pltpu.make_async_copy(source, upd.at[chip], back_recv).start()

    each(PART // TILE, scale)

    for way in (0, 1):
        sent_raw = own.at[0]
        pltpu.make_async_copy(sent_raw, sent_raw, raw_send.at[way]).wait()
        pltpu.make_async_copy(codes_out.at[way], codes_out.at[way], code_send.at[way]).wait()
        pltpu.make_async_copy(units_out.at[way], units_out.at[way], unit_send.at[way]).wait()
    swap_half(0).wait_send()
    swap_half(1).wait_send()
    here = gathered.at[core]
    pltpu.make_async_copy(here, here, pair_send).wait()
    sent = back.at[pl.ds(0, HALF - 1)]
    pltpu.make_async_copy(sent, sent, row_send).wait()
    sent_sums = sums_in.at[pl.ds(0, OWNERS - 1)]
    pltpu.make_async_copy(sent_sums, sent_sums, sum_send).wait()
    moment_copy.wait()
    returns = lax.div(me, HALF) == core

    @pl.when(returns)
    def _():
        sent_back = back.at[pl.ds(0, HALF - 1)]
        pltpu.make_async_copy(sent_back, sent_back, back_send).wait()

    @pl.when(jnp.logical_not(returns))
    def _():
        pltpu.make_async_copy(back, back, back_send).wait()

    pltpu.make_async_copy(back, upd, back_recv).wait()


def write_out(upd, moment_in, update, moment, upd_v, update_v, moment_v, sems):
    rows_in = pltpu.make_async_copy(upd, upd_v, sems.at[0])
    moment_here = pltpu.make_async_copy(moment_in, moment_v, sems.at[1])
    rows_in.start()
    moment_here.start()
    moment_here.wait()
    moment_out = pltpu.make_async_copy(moment_v, moment, sems.at[2])
    moment_out.start()
    rows_in.wait()
    wide = upd_v[...].astype(F32)
    for c in range(4):
        update_v[:, :, c * LANES:(c + 1) * LANES] = wide[:, c * ROWS:(c + 1) * ROWS].astype(BF16)
    rows_out = pltpu.make_async_copy(update_v, update, sems.at[3])
    rows_out.start()
    moment_out.wait()
    rows_out.wait()


def on_device(gradients, statistics, newton_steps, second_moment):
    chunk = (COLS, ROWS, SIZE)
    dma = pltpu.SemaphoreType.DMA
    square_f = pltpu.VMEM((SIZE, SIZE), F32)
    square_b = pltpu.VMEM((SIZE, SIZE), BF16)
    left = pltpu.VMEM((SIZE, 3 * SIZE), BF16)
    right = pltpu.VMEM((3 * SIZE, SIZE), BF16)
    anywhere = pl.BlockSpec(memory_space=pl.ANY)
    group_f = pltpu.VMEM((COLS, RINGS, ROWS, SIZE), F32)
    upd, moment = pl.pallas_call(
        kernel,
        out_shape=(
            jax.ShapeDtypeStruct((HALF, 32, LANES), BF16),
            jax.ShapeDtypeStruct((COLS, RINGS, ROWS, SIZE), F32),
        ),
        in_specs=[anywhere] * 4,
        out_specs=(anywhere, anywhere),
        scratch_shapes=[
            pltpu.VMEM((WAYS, COLS, RINGS, ROWS, SIZE), BF16),
            square_f,
            group_f,
            group_f,
            pltpu.VMEM((2, 4) + chunk, BF16),
            pltpu.VMEM((2, 4) + chunk, BF16),
            pltpu.VMEM((2, 20) + chunk, jnp.int16),
            pltpu.VMEM((2, 20) + chunk, jnp.int16),
            pltpu.VMEM((2, 20, COLS, 1, LANES), F32),
            pltpu.VMEM((2, 20, COLS, 1, LANES), F32),
            pltpu.SMEM((1,), jnp.int32),
            pltpu.VMEM((RINGS, COLS, 32, LANES), BF16),
            pltpu.VMEM((2, RINGS, COLS, 32, LANES), BF16),
            pltpu.VMEM((RINGS, COLS, 1, LANES), F32),
            pltpu.VMEM((OWNERS, 1, LANES), F32),
            square_b,
            square_b,
            pltpu.VMEM((HALF, 32, LANES), BF16),
            pltpu.VMEM((2, 2, SIZE, PART), BF16),
        ]
        + [square_f] * 5
        + [left] * 5
        + [right] * 3
        + [
            dma((5,)), dma((2,)), dma((2, 8)), dma((2,)), dma((2, 20)), dma((2,)), dma((2, 20)),
            dma, dma((8,)), dma, dma,
            dma, dma, dma((2,)), dma((2,)), dma, dma,
        ],
        compiler_params=pltpu.CompilerParams(
            collective_id=0, has_side_effects=True, vmem_limit_bytes=56 * 2**20
        ),
    )(
        gradients.reshape(WAYS, COLS, RINGS, ROWS, SIZE),
        statistics.reshape(SIZE, SIZE),
        newton_steps,
        second_moment.reshape(COLS, RINGS, ROWS, SIZE),
    )
    return pl.pallas_call(
        write_out,
        out_shape=(
            jax.ShapeDtypeStruct((HALF, ROWS, SIZE), BF16),
            jax.ShapeDtypeStruct((HALF, ROWS, SIZE), F32),
        ),
        in_specs=[anywhere, anywhere],
        out_specs=(anywhere, anywhere),
        scratch_shapes=[
            pltpu.VMEM((HALF, 32, LANES), BF16),
            pltpu.VMEM((HALF, ROWS, SIZE), BF16),
            pltpu.VMEM((HALF, ROWS, SIZE), F32),
            dma((4,)),
        ],
    )(upd, moment.reshape(HALF, ROWS, SIZE))


def solution(mesh):
    return jax.shard_map(
        on_device,
        mesh=mesh,
        in_specs=(
            P("dp", None, "fsdp", None),
            P(("dp", "fsdp"), None, None),
            P(("dp", "fsdp")),
            P("dp", "fsdp", None),
        ),
        out_specs=(P("dp", "fsdp", None), P("dp", "fsdp", None)),
        check_vma=False,
    )
```

```python
import jax
import jax.numpy as jnp
from jax import lax
from jax.experimental import pallas as pl
from jax.experimental.pallas import tpu as pltpu
from jax.sharding import PartitionSpec as P

stat_decay = 0.9
moment_decay = 0.95
adam_eps = 1e-08
ratio_eps = 1e-06
MESH = pl.DeviceIdType.MESH
F32 = jnp.float32
BF16 = jnp.bfloat16
LANES = 128
ROWS = 8
TILE = 64
SIZE = 512
WAYS = 8
COLS = 4
RINGS = 8
OWNERS = 64
HALF = OWNERS // 2
PART = 256
FAR = 7


def kernel(
    grad, stats, steps, second, upd, moment,
    own, stat_v, second_v, moment_v,
    r1, leaf, codes_out, codes_in, units_out, units_in, steps_v,
    outgoing, gathered, sums_out, sums_in, adam_pair, block, middle, back, roots,
    a_f, p_f, q_f, m_f, n_f,
    a_b, b_b, p_b, n_b, m_b,
    local_sem, raw_send, raw_recv, code_send, unit_send, sum_over_recv, row_send, row_recv, cross_send, cross_recv,
    pair_send, pair_recv, sum_send, sum_recv, sum_pair_send, sum_pair_recv, root_send, root_recv,
    back_send, back_recv,
):
    y = lax.axis_index("dp")
    me = lax.axis_index("fsdp")
    core = lax.rem(me, 2)
    chip = lax.div(me, 2)
    x = lax.div(chip, RINGS)
    z = lax.rem(chip, RINGS)
    partner = me + 1 - 2 * core

    def each(count, fn, first=0):
        def one(j, carry):
            fn(j)
            return carry

        lax.fori_loop(first, count, one, 0)

    barrier = pltpu.get_barrier_semaphore()
    for shift in (1, WAYS - 1):
        pl.semaphore_signal(
            barrier, inc=1, device_id={"dp": lax.rem(y + shift, WAYS)}, device_id_type=MESH
        )

    def hello(target):
        pl.semaphore_signal(barrier, inc=1, device_id={"fsdp": target}, device_id_type=MESH)

    for turn in range(1, COLS):
        hello(lax.rem(me + 2 * RINGS * turn, OWNERS))

    def greet(t):
        low = lax.rem(me + t, 2 * RINGS)
        for high in range(COLS):
            hello(2 * RINGS * high + low)

    each(2 * RINGS, greet, 1)
    own_copy = pltpu.make_async_copy(grad, own, local_sem.at[0])
    stat_copy = pltpu.make_async_copy(stats, stat_v, local_sem.at[1])
    second_copy = pltpu.make_async_copy(second, second_v, local_sem.at[2])
    steps_copy = pltpu.make_async_copy(steps, steps_v, local_sem.at[4])
    own_copy.start()
    second_copy.start()
    stat_copy.start()
    steps_copy.start()
    pl.semaphore_wait(barrier, OWNERS + 1)

    def group(way, distance):
        return lax.rem(y + (distance if way == 0 else WAYS - distance), WAYS)

    def shift_of(place):
        half = lax.div(place + 1, 2)
        return 4 + half * (1 - 2 * lax.rem(place, 2))

    def column(place):
        return lax.rem(z + shift_of(place), RINGS)

    def ring(way, source, target, send, recv):
        return pltpu.make_async_remote_copy(
            src_ref=source,
            dst_ref=target,
            send_sem=send,
            recv_sem=recv,
            device_id={"dp": group(way, 1)},
            device_id_type=MESH,
        )

    def raw(way, index, distance, place, target):
        source = grad.at[group(way, distance), :, column(place)]
        return ring(way, source, target, raw_send.at[way], raw_recv.at[way, index])

    def long_place(way, batch, i):
        return 4 * batch + 2 * way + i

    def short_place(way, batch, i):
        return 4 * batch + 2 * (1 - way) + i

    def hop1(way, batch, i):
        index = 2 * batch + i
        return raw(way, index, 4, long_place(way, batch, i), r1.at[way, index])

    def hop2_leaf(way, batch, i):
        index = 2 * batch + i
        return raw(way, 4 + index, 3, short_place(way, batch, i), leaf.at[way, index])

    def codes(way, index):
        return ring(
            way, codes_out.at[way, index], codes_in.at[way, index], code_send.at[way], sum_over_recv.at[way, index]
        )

    def units(way, index):
        return ring(
            way, units_out.at[way, index], units_in.at[way, index], unit_send.at[way], sum_over_recv.at[way, index]
        )

    def near_power(value):
        wide = value * (2.0**23 + 1.0)
        return wide - (wide - value)

    def columns_of(value):
        return [value[:, :, c * LANES:(c + 1) * LANES] for c in range(4)]

    def send_sum(way, index, value):
        parts = columns_of(value)
        size = [jnp.abs(part) for part in parts]
        largest = jnp.maximum(jnp.maximum(size[0], size[1]), jnp.maximum(size[2], size[3]))
        largest = jnp.maximum(jnp.max(largest, axis=1, keepdims=True), 1e-25)
        power = near_power(largest)
        units_out[way, index] = power * 2.0**-14
        units(way, index).start()
        inverse = near_power(2.0**14 / power)
        near = [(part * inverse + 1.5 * 2.0**23) - 1.5 * 2.0**23 for part in parts]
        codes_out[way, index] = jnp.concatenate(near, axis=2).astype(jnp.int32).astype(jnp.int16)
        codes(way, index).start()

    def received(way, index):
        both = units_in.at[0, pl.ds(0, 17)]
        pltpu.make_async_copy(both, both, sum_over_recv.at[way, index]).wait()
        unit = units_in[way, index]
        parts = columns_of(codes_in[way, index].astype(jnp.int32).astype(F32))
        return jnp.concatenate([part * unit for part in parts], axis=2)

    def mine(way, distance, place):
        return own[group(way, distance), :, column(place)].astype(F32)

    def both_ways(batch, fn):
        def one(i):
            for way in (0, 1):
                fn(way, batch, i)

        each(2, one)

    def start1(way, batch, i):
        hop1(way, batch, i).start()

    def start2_leaf(way, batch, i):
        hop2_leaf(way, batch, i).start()

    def start2(way, batch, i):
        index = 2 * batch + i
        hop1(way, batch, i).wait_recv()
        send_sum(way, index, r1[way, index].astype(F32) + mine(way, 3, long_place(way, batch, i)))

    def short3(way, batch, i):
        place = short_place(way, batch, i)
        hop2_leaf(way, batch, i).wait_recv()
        send_sum(way, 4 + place, leaf[way, 2 * batch + i].astype(F32) + mine(way, 2, place))

    def long3(way, batch, i):
        place = long_place(way, batch, i)
        send_sum(way, 4 + place, received(way, 2 * batch + i) + mine(way, 2, place))

    def last4(way, place):
        send_sum(way, 12 + place, received(way, 4 + place) + mine(way, 1, place))

    def short4(way, batch, i):
        last4(way, short_place(way, batch, i))

    def long4(way, batch, i):
        last4(way, long_place(way, batch, i))

    def finish(place):
        col = column(place)
        total = received(0, 12 + place) + received(1, 12 + place) + own[y, :, col].astype(F32)
        mean = total * (1.0 / WAYS)
        new = moment_decay * second_v[:, col] + (1.0 - moment_decay) * mean * mean
        moment_v[:, col] = new
        adam = mean / (jnp.sqrt(new) + adam_eps)
        square = adam * adam
        squares = columns_of(square)
        outgoing[place] = jnp.concatenate(columns_of(mean), axis=1).astype(BF16)
        sums_out[place] = jnp.sum(
            (squares[0] + squares[1]) + (squares[2] + squares[3]), axis=1, keepdims=True
        )
        for index in range(COLS):
            to_owner(
                2 * (index * RINGS + col) + core,
                outgoing.at[place, index],
                gathered.at[core, place, x],
                row_send,
                row_recv.at[place],
            )

    def to_owner(target, source, there, send, recv):
        @pl.when(target != me)
        def _():
            pltpu.make_async_remote_copy(
                src_ref=source,
                dst_ref=there,
                send_sem=send,
                recv_sem=recv,
                device_id={"fsdp": target},
                device_id_type=MESH,
            ).start()

        @pl.when(target == me)
        def _():
            pltpu.make_async_copy(source, there, recv).start()

    def finish_near(place):
        finish(place)
        for index in range(COLS):
            pltpu.make_async_remote_copy(
                src_ref=outgoing.at[place, index],
                dst_ref=gathered.at[core, place, x],
                send_sem=cross_send,
                recv_sem=cross_recv,
                device_id={"fsdp": 2 * (index * RINGS + column(place)) + 1 - core},
                device_id_type=MESH,
            ).start()

    both_ways(0, start1)
    both_ways(0, start2_leaf)
    both_ways(1, start1)
    own_copy.wait()
    both_ways(0, start2)
    both_ways(0, short3)
    both_ways(1, start2_leaf)
    both_ways(0, long3)
    both_ways(0, short4)
    both_ways(1, start2)
    both_ways(0, long4)
    both_ways(1, short3)
    both_ways(1, long3)
    second_copy.wait()
    each(4, finish)
    both_ways(1, short4)
    both_ways(1, long4)
    each(FAR, finish, 4)
    each(RINGS, finish_near, FAR)
    moment_copy = pltpu.make_async_copy(moment_v, moment, local_sem.at[3])
    moment_copy.start()

    def to_partner(source, target, send, recv):
        return pltpu.make_async_remote_copy(
            src_ref=source,
            dst_ref=target,
            send_sem=send,
            recv_sem=recv,
            device_id={"fsdp": partner},
            device_id_type=MESH,
        )

    def forward(place):
        here = gathered.at[core, place]
        pltpu.make_async_copy(here, here, row_recv.at[place]).wait()
        to_partner(here, here, pair_send, pair_recv).start()

    def send_adam(place):
        for index in range(COLS):
            to_owner(
                2 * (index * RINGS + column(place)) + core,
                sums_out.at[place, index],
                sums_in.at[chip],
                sum_send,
                sum_recv,
            )

    each(RINGS, send_adam)
    each(FAR, forward)

    stat_copy.wait()
    for place in range(FAR, RINGS):
        here = gathered.at[core, place]
        pltpu.make_async_copy(here, here, row_recv.at[place]).wait()
    near = gathered.at[1 - core, pl.ds(FAR, RINGS - FAR)]
    pltpu.make_async_copy(near, near, cross_recv).wait()
    there = gathered.at[1 - core, pl.ds(0, FAR)]
    pltpu.make_async_copy(there, there, pair_recv).wait()

    def assemble(place):
        source_z = lax.rem(z + RINGS - shift_of(place) + RINGS, RINGS)
        for index in range(COLS):
            pair = [gathered[c, place, index].astype(F32) for c in (0, 1)]
            start = pl.multiple_of((index * RINGS + source_z) * 16, 16)
            for c in range(4):
                both = [p[c * ROWS:(c + 1) * ROWS] for p in pair]
                block[pl.ds(start, 16), c * LANES:(c + 1) * LANES] = jnp.concatenate(both, axis=0).astype(BF16)

    each(8, assemble)

    @pl.when(core == 0)
    def _():
        p_f[...] = lax.dot_general(
            block[...], block[...], (((1,), (1,)), ((), ())), preferred_element_type=F32
        )

    @pl.when(core == 1)
    def _():
        p_f[...] = lax.dot_general(
            block[...], block[...], (((0,), (0,)), ((), ())), preferred_element_type=F32
        )

    def square_sum(value):
        return jnp.sum((value * value).reshape(value.shape[0] // ROWS, ROWS, value.shape[1]), axis=0)

    def halves(value):
        high = value.astype(BF16)
        return high, (value - high.astype(F32)).astype(BF16)

    def put(ref, here, value):
        high, low = halves(value)
        ref[(0,) + here] = high
        ref[(1,) + here] = low

    def three(left, right, rows, cols):
        def one(a, b):
            return jnp.dot(left[a, rows], right[b, :, cols], preferred_element_type=F32)

        return one(0, 0) + one(1, 0) + one(0, 1)

    low, high = slice(0, PART), slice(PART, SIZE)

    def product(left, right, use):
        def spread(piece, rows, cols):
            for t in range(0, PART, TILE):
                here = slice(rows.start + t, rows.start + t + TILE)
                use(here.start, cols, (here, cols), piece[t:t + TILE])

        corner = three(left, right, low, low)
        side = three(left, right, low, high)
        spread(corner, low, low)
        end = three(left, right, high, high)
        spread(side, low, high)
        spread(side.T, high, low)
        spread(end, high, high)

    def identity(t, cols, scale):
        shape = (TILE, cols.stop - cols.start)
        row = lax.broadcasted_iota(jnp.int32, shape, 0) + t
        lane = lax.broadcasted_iota(jnp.int32, shape, 1) + cols.start
        return jnp.where(row == lane, scale, 0.0)

    everything = slice(0, SIZE)
    norm = jnp.zeros((ROWS, SIZE), F32)
    for t in range(0, SIZE, TILE):
        here = slice(t, t + TILE)
        value = stat_decay * stat_v[here] + (1.0 - stat_decay) * p_f[here]
        a_f[here] = value
        norm = norm + square_sum(value)
        put(a_b, (here, everything), value)
    frobenius = jnp.sqrt(jnp.sum(norm, keepdims=True))
    scaling = 5.0 / (2.0 * frobenius)
    first = jnp.sqrt(jnp.sqrt(scaling))

    def squared(t, cols, here, q):
        value = (q * scaling) * scaling
        p_f[here] = value
        put(b_b, here, 0.0625 * value - (0.625 * scaling) * a_f[here])
        put(p_b, here, value)

    def cubed(t, cols, here, q):
        value = (1.5625 * scaling) * a_f[here] - 0.625 * p_f[here] + (0.0625 * scaling) * q
        n_f[here] = value
        put(n_b, here, value)

    def moved(t, cols, here, q):
        value = 1.5625 * n_f[here] + q
        m_f[here] = value
        put(m_b, here, value)

    def squared_again(t, cols, here, q):
        m = m_f[here]
        value = 1.25 * m - 0.25 * q
        n_f[here] = value
        put(n_b, here, value)
        put(b_b, here, 0.0625 * q - 0.625 * m)

    def fourth(t, cols, here, q):
        value = 1.5625 * n_f[here] + q
        p_f[here] = value
        put(p_b, here, value)

    steps_copy.wait()
    count = steps_v[0]

    def last_factor(t, cols, here, q):
        second_w = identity(t, cols, 1.25) - 0.25 * m_f[here]
        third = 1.25 * second_w - 0.25 * (1.5625 * p_f[here] + q)
        value = jnp.where(count == 2, second_w, third)
        n_f[here] = value
        put(n_b, here, value)

    def swap_half(h):
        here = roots.at[core, h]
        return to_partner(here, here, root_send.at[h], root_recv.at[h])

    def swapped_half(h):
        here = roots.at[1 - core, h]
        return to_partner(here, here, root_send.at[h], root_recv.at[h])

    def choose(t, cols, here, q):
        one = identity(t, cols, 1.25) - (0.25 * scaling) * a_f[here]
        more = 1.25 * n_f[here] - (0.25 * scaling) * q
        value = jnp.where(count == 1, one, more)
        h = cols.start // PART
        roots[core, h, t:t + TILE] = (first * value).astype(BF16)
        if t + TILE == SIZE:
            swap_half(h).start()

    product(a_b, a_b, squared)
    product(a_b, p_b, cubed)
    product(b_b, n_b, moved)
    product(m_b, m_b, squared_again)
    product(n_b, b_b, fourth)
    product(p_b, b_b, last_factor)

    for cols in (low, high):
        last = three(a_b, n_b, slice(0, SIZE), cols)
        for t in range(0, SIZE, TILE):
            choose(t, cols, (slice(t, t + TILE), cols), last[t:t + TILE])

    pltpu.make_async_copy(sums_in, sums_in, sum_recv).wait()
    adam_pair[core] = jnp.sum(sums_in[...], axis=0)
    adam_swap = to_partner(adam_pair.at[core], adam_pair.at[core], sum_pair_send, sum_pair_recv)
    adam_swapped = to_partner(adam_pair.at[1 - core], adam_pair.at[1 - core], sum_pair_send, sum_pair_recv)
    adam_swap.start()
    @pl.when(core == 1)
    def _():
        swapped_half(0).wait_recv()

    total = jnp.dot(roots[0, 0], block[0:PART], preferred_element_type=F32)

    @pl.when(core == 1)
    def _():
        swapped_half(1).wait_recv()

    total = total + jnp.dot(roots[0, 1], block[PART:SIZE], preferred_element_type=F32)
    middle[...] = total.astype(BF16)

    dir_sq = jnp.zeros((ROWS, PART), F32)
    for h in (0, 1):
        @pl.when(core == 0)
        def _():
            swapped_half(h).wait_recv()

        cols = slice(h * PART, (h + 1) * PART)
        q_f[:, cols] = jnp.dot(middle[...], roots[1, h], preferred_element_type=F32)
        for t in range(0, SIZE, TILE):
            here = slice(t, t + TILE)
            value = q_f[here, cols].astype(BF16).astype(F32)
            q_f[here, cols] = value
            dir_sq = dir_sq + square_sum(value)
    dir_sq = jnp.sum(dir_sq, keepdims=True)
    adam_swapped.wait_recv()
    adam_sq = jnp.sum(adam_pair[0] + adam_pair[1], keepdims=True)
    ratio = jnp.sqrt(adam_sq) / (jnp.sqrt(dir_sq) + ratio_eps)

    for t in range(PART // TILE):
        here = pl.ds(pl.multiple_of(core * PART + t * TILE, TILE), TILE)
        value = q_f[here] * ratio
        parts = [
            value[:, c * LANES:(c + 1) * LANES].reshape(TILE // ROWS, ROWS, LANES) for c in range(4)
        ]
        back[t * 8:(t + 1) * 8] = jnp.concatenate(parts, axis=1).astype(BF16)

    def give(row):
        for index in range(COLS):
            slot = 2 * (index // 2 * RINGS + row) + index % 2
            to_owner(core * HALF + slot, back.at[slot], upd.at[chip], back_send, back_recv)

    each(RINGS, give)

    for way in (0, 1):
        sent_raw = own.at[0]
        pltpu.make_async_copy(sent_raw, sent_raw, raw_send.at[way]).wait()
        pltpu.make_async_copy(codes_out.at[way], codes_out.at[way], code_send.at[way]).wait()
        pltpu.make_async_copy(units_out.at[way], units_out.at[way], unit_send.at[way]).wait()
    swap_half(0).wait_send()
    swap_half(1).wait_send()
    here = gathered.at[core, pl.ds(0, FAR)]
    pltpu.make_async_copy(here, here, pair_send).wait()
    here = gathered.at[core, pl.ds(0, RINGS - FAR)]
    pltpu.make_async_copy(here, here, cross_send).wait()
    sent = back.at[pl.ds(0, HALF - 1)]
    pltpu.make_async_copy(sent, sent, row_send).wait()
    sent_sums = sums_in.at[pl.ds(0, HALF - 1)]
    pltpu.make_async_copy(sent_sums, sent_sums, sum_send).wait()
    adam_swap.wait_send()
    moment_copy.wait()
    returns = lax.div(me, HALF) == core

    @pl.when(returns)
    def _():
        sent_back = back.at[pl.ds(0, HALF - 1)]
        pltpu.make_async_copy(sent_back, sent_back, back_send).wait()

    @pl.when(jnp.logical_not(returns))
    def _():
        pltpu.make_async_copy(back, back, back_send).wait()

    pltpu.make_async_copy(back, upd, back_recv).wait()


def write_out(upd, moment_in, update, moment, upd_v, update_v, moment_v, sems):
    def quarter(t):
        return pl.ds(t * 8, 8)

    def come(t):
        here = quarter(t)
        return (
            pltpu.make_async_copy(moment_in.at[here], moment_v.at[here], sems.at[t]),
            pltpu.make_async_copy(upd.at[here], upd_v.at[here], sems.at[4 + t]),
        )

    def go(t):
        here = quarter(t)
        return (
            pltpu.make_async_copy(moment_v.at[here], moment.at[here], sems.at[8 + t]),
            pltpu.make_async_copy(update_v.at[here], update.at[here], sems.at[12 + t]),
        )

    coming = [come(t) for t in range(4)]
    going = [go(t) for t in range(4)]
    for pair in coming:
        for copy in pair:
            copy.start()
    for t in range(4):
        coming[t][0].wait()
        going[t][0].start()
        coming[t][1].wait()
        wide = upd_v[t * 8:(t + 1) * 8].astype(F32)
        for c in range(4):
            update_v[t * 8:(t + 1) * 8, :, c * LANES:(c + 1) * LANES] = wide[:, c * ROWS:(c + 1) * ROWS].astype(BF16)
        going[t][1].start()
    for pair in going:
        for copy in pair:
            copy.wait()


def on_device(gradients, statistics, newton_steps, second_moment):
    chunk = (COLS, ROWS, SIZE)
    dma = pltpu.SemaphoreType.DMA
    square_f = pltpu.VMEM((SIZE, SIZE), F32)
    square_b = pltpu.VMEM((SIZE, SIZE), BF16)
    both = pltpu.VMEM((2, SIZE, SIZE), BF16)
    anywhere = pl.BlockSpec(memory_space=pl.ANY)
    group_f = pltpu.VMEM((COLS, RINGS, ROWS, SIZE), F32)
    upd, moment = pl.pallas_call(
        kernel,
        out_shape=(
            jax.ShapeDtypeStruct((HALF, 32, LANES), BF16),
            jax.ShapeDtypeStruct((COLS, RINGS, ROWS, SIZE), F32),
        ),
        in_specs=[anywhere] * 4,
        out_specs=(anywhere, anywhere),
        scratch_shapes=[
            pltpu.VMEM((WAYS, COLS, RINGS, ROWS, SIZE), BF16),
            square_f,
            group_f,
            group_f,
            pltpu.VMEM((2, 4) + chunk, BF16),
            pltpu.VMEM((2, 4) + chunk, BF16),
            pltpu.VMEM((2, 20) + chunk, jnp.int16),
            pltpu.VMEM((2, 20) + chunk, jnp.int16),
            pltpu.VMEM((2, 20, COLS, 1, LANES), F32),
            pltpu.VMEM((2, 20, COLS, 1, LANES), F32),
            pltpu.SMEM((1,), jnp.int32),
            pltpu.VMEM((RINGS, COLS, 32, LANES), BF16),
            pltpu.VMEM((2, RINGS, COLS, 32, LANES), BF16),
            pltpu.VMEM((RINGS, COLS, 1, LANES), F32),
            pltpu.VMEM((HALF, 1, LANES), F32),
            pltpu.VMEM((2, 1, LANES), F32),
            square_b,
            square_b,
            pltpu.VMEM((HALF, 32, LANES), BF16),
            pltpu.VMEM((2, 2, SIZE, PART), BF16),
        ]
        + [square_f] * 5
        + [both] * 5
        + [
            dma((5,)), dma((2,)), dma((2, 8)), dma((2,)), dma((2,)), dma((2, 20)), dma, dma((8,)), dma, dma,
            dma, dma, dma, dma, dma, dma, dma((2,)), dma((2,)), dma, dma,
        ],
        compiler_params=pltpu.CompilerParams(
            collective_id=0, has_side_effects=True, vmem_limit_bytes=56 * 2**20
        ),
    )(
        gradients.reshape(WAYS, COLS, RINGS, ROWS, SIZE),
        statistics.reshape(SIZE, SIZE),
        newton_steps,
        second_moment.reshape(COLS, RINGS, ROWS, SIZE),
    )
    return pl.pallas_call(
        write_out,
        out_shape=(
            jax.ShapeDtypeStruct((HALF, ROWS, SIZE), BF16),
            jax.ShapeDtypeStruct((HALF, ROWS, SIZE), F32),
        ),
        in_specs=[anywhere, anywhere],
        out_specs=(anywhere, anywhere),
        scratch_shapes=[
            pltpu.VMEM((HALF, 32, LANES), BF16),
            pltpu.VMEM((HALF, ROWS, SIZE), BF16),
            pltpu.VMEM((HALF, ROWS, SIZE), F32),
            dma((16,)),
        ],
    )(upd, moment.reshape(HALF, ROWS, SIZE))


def solution(mesh):
    return jax.shard_map(
        on_device,
        mesh=mesh,
        in_specs=(
            P("dp", None, "fsdp", None),
            P(("dp", "fsdp"), None, None),
            P(("dp", "fsdp")),
            P("dp", "fsdp", None),
        ),
        out_specs=(P("dp", "fsdp", None), P("dp", "fsdp", None)),
        check_vma=False,
    )
```

```python
import jax
import jax.numpy as jnp
from jax import lax
from jax.experimental import pallas as pl
from jax.experimental.pallas import tpu as pltpu
from jax.sharding import PartitionSpec as P

stat_decay = 0.9
moment_decay = 0.95
adam_eps = 1e-08
ratio_eps = 1e-06
MESH = pl.DeviceIdType.MESH
F32 = jnp.float32
BF16 = jnp.bfloat16
LANES = 128
ROWS = 8
TILE = 64
SIZE = 512
WAYS = 8
COLS = 4
RINGS = 8
OWNERS = 64
HALF = OWNERS // 2
PART = 256
FAR = 7


def kernel(
    grad, stats, steps, second, upd, moment,
    own, stat_v, second_v, moment_v,
    r1, leaf, codes_out, codes_in, units_out, units_in, sized, steps_v,
    outgoing, gathered, sums_out, sums_in, adam_pair, block, middle, back, roots,
    a_f, p_f, q_f, m_f, n_f,
    a_b, b_b, p_b, n_b, m_b,
    local_sem, raw_send, raw_recv, code_send, unit_send, sum_over_recv, row_send, row_recv, cross_send, cross_recv,
    pair_send, pair_recv, sum_send, sum_recv, sum_pair_send, sum_pair_recv, root_send, root_recv,
    back_send, back_recv,
):
    y = lax.axis_index("dp")
    me = lax.axis_index("fsdp")
    core = lax.rem(me, 2)
    chip = lax.div(me, 2)
    x = lax.div(chip, RINGS)
    z = lax.rem(chip, RINGS)
    partner = me + 1 - 2 * core

    def each(count, fn, first=0):
        def one(j, carry):
            fn(j)
            return carry

        lax.fori_loop(first, count, one, 0)

    barrier = pltpu.get_barrier_semaphore()
    for shift in (1, WAYS - 1):
        pl.semaphore_signal(
            barrier, inc=1, device_id={"dp": lax.rem(y + shift, WAYS)}, device_id_type=MESH
        )

    def hello(target):
        pl.semaphore_signal(barrier, inc=1, device_id={"fsdp": target}, device_id_type=MESH)

    def greet(k):
        t = RINGS + lax.div(k + 1, 2) * (1 - 2 * lax.rem(k, 2))
        low = lax.rem(me + t, 2 * RINGS)
        for high in range(COLS):
            hello(2 * RINGS * high + low)

    each(2 * RINGS - 1, greet)
    for turn in range(1, COLS):
        hello(lax.rem(me + 2 * RINGS * turn, OWNERS))

    own_copy = pltpu.make_async_copy(grad, own, local_sem.at[0])
    stat_copy = pltpu.make_async_copy(stats, stat_v, local_sem.at[1])
    second_copy = pltpu.make_async_copy(second, second_v, local_sem.at[2])
    steps_copy = pltpu.make_async_copy(steps, steps_v, local_sem.at[4])
    own_copy.start()
    second_copy.start()
    stat_copy.start()
    steps_copy.start()
    pl.semaphore_wait(barrier, OWNERS + 1)

    def group(way, distance):
        return lax.rem(y + (distance if way == 0 else WAYS - distance), WAYS)

    def shift_of(place):
        half = lax.div(place + 1, 2)
        return 4 + half * (1 - 2 * lax.rem(place, 2))

    def column(place):
        return lax.rem(z + shift_of(place), RINGS)

    def ring(way, source, target, send, recv):
        return pltpu.make_async_remote_copy(
            src_ref=source,
            dst_ref=target,
            send_sem=send,
            recv_sem=recv,
            device_id={"dp": group(way, 1)},
            device_id_type=MESH,
        )

    def raw(way, index, distance, place, target):
        source = grad.at[group(way, distance), :, column(place)]
        return ring(way, source, target, raw_send.at[way], raw_recv.at[way, index])

    def long_place(way, batch, i):
        return 4 * batch + 2 * way + i

    def short_place(way, batch, i):
        return 4 * batch + 2 * (1 - way) + i

    def hop1(way, batch, i):
        index = 2 * batch + i
        return raw(way, index, 4, long_place(way, batch, i), r1.at[way, index])

    def hop2_leaf(way, batch, i):
        index = 2 * batch + i
        return raw(way, 4 + index, 3, short_place(way, batch, i), leaf.at[way, index])

    lane = lax.broadcasted_iota(jnp.int32, (1, 1, LANES), 2)

    def codes(way, index):
        return ring(
            way, codes_out.at[way, index], codes_in.at[way, index], code_send.at[way], sum_over_recv.at[way, index]
        )

    def units(way, index):
        return ring(
            way, units_out.at[way, index], units_in.at[way, index], unit_send.at[way], sum_over_recv.at[way, index]
        )

    def near_power(value):
        wide = value * (2.0**23 + 1.0)
        return wide - (wide - value)

    def columns_of(value):
        return [value[:, :, c * LANES:(c + 1) * LANES] for c in range(4)]

    def send_sum(way, index, value):
        parts = columns_of(value)
        size = [jnp.abs(part) for part in parts]
        largest = jnp.maximum(jnp.maximum(size[0], size[1]), jnp.maximum(size[2], size[3]))
        largest = jnp.maximum(largest, pltpu.roll(largest, LANES // 2, 2))
        largest = jnp.maximum(jnp.max(largest, axis=1, keepdims=True), 1e-25)
        power = near_power(largest)
        units_out[way, index] = jnp.where(lane < LANES // 2, power[0:2], power[2:4]) * 2.0**-14
        units(way, index).start()
        inverse = near_power(2.0**14 / power)
        near = [(part * inverse + 1.5 * 2.0**23) - 1.5 * 2.0**23 for part in parts]
        codes_out[way, index] = jnp.concatenate(near, axis=2).astype(jnp.int32).astype(jnp.int16)
        codes(way, index).start()

    def received(way, index):
        pltpu.make_async_copy(sized, sized, sum_over_recv.at[way, index]).wait()
        here = jnp.broadcast_to(units_in[way, index], (2, ROWS, LANES))
        there = pltpu.roll(here, LANES // 2, 2)
        unit = jnp.concatenate(
            [jnp.where(lane < LANES // 2, here, there), jnp.where(lane < LANES // 2, there, here)], axis=0
        )
        parts = columns_of(codes_in[way, index].astype(jnp.int32).astype(F32))
        return jnp.concatenate([part * unit for part in parts], axis=2)

    def mine(way, distance, place):
        return own[group(way, distance), :, column(place)].astype(F32)

    def both_ways(batch, fn):
        def one(i):
            for way in (0, 1):
                fn(way, batch, i)

        each(2, one)

    def start1(way, batch, i):
        hop1(way, batch, i).start()

    def start2_leaf(way, batch, i):
        hop2_leaf(way, batch, i).start()

    def start2(way, batch, i):
        index = 2 * batch + i
        hop1(way, batch, i).wait_recv()
        send_sum(way, index, r1[way, index].astype(F32) + mine(way, 3, long_place(way, batch, i)))

    def short3(way, batch, i):
        place = short_place(way, batch, i)
        hop2_leaf(way, batch, i).wait_recv()
        send_sum(way, 4 + place, leaf[way, 2 * batch + i].astype(F32) + mine(way, 2, place))

    def long3(way, batch, i):
        place = long_place(way, batch, i)
        send_sum(way, 4 + place, received(way, 2 * batch + i) + mine(way, 2, place))

    def last4(way, place):
        send_sum(way, 12 + place, received(way, 4 + place) + mine(way, 1, place))

    def short4(way, batch, i):
        last4(way, short_place(way, batch, i))

    def long4(way, batch, i):
        last4(way, long_place(way, batch, i))

    def finish(place):
        col = column(place)
        total = received(0, 12 + place) + received(1, 12 + place) + own[y, :, col].astype(F32)
        mean = total * (1.0 / WAYS)
        new = moment_decay * second_v[:, col] + (1.0 - moment_decay) * mean * mean
        moment_v[:, col] = new
        adam = mean / (jnp.sqrt(new) + adam_eps)
        square = adam * adam
        squares = columns_of(square)
        outgoing[place] = jnp.concatenate(columns_of(mean), axis=1).astype(BF16)
        sums_out[place] = jnp.sum(
            (squares[0] + squares[1]) + (squares[2] + squares[3]), axis=1, keepdims=True
        )
        for turn in (2, 1, 3, 0):
            index = lax.rem(x + turn, COLS)
            to_owner(
                2 * (index * RINGS + col) + core,
                outgoing.at[place, index],
                gathered.at[core, place, x],
                row_send,
                row_recv.at[place],
            )

    def to_owner(target, source, there, send, recv):
        @pl.when(target != me)
        def _():
            pltpu.make_async_remote_copy(
                src_ref=source,
                dst_ref=there,
                send_sem=send,
                recv_sem=recv,
                device_id={"fsdp": target},
                device_id_type=MESH,
            ).start()

        @pl.when(target == me)
        def _():
            pltpu.make_async_copy(source, there, recv).start()

    def finish_near(place):
        finish(place)
        for index in range(COLS):
            pltpu.make_async_remote_copy(
                src_ref=outgoing.at[place, index],
                dst_ref=gathered.at[core, place, x],
                send_sem=cross_send,
                recv_sem=cross_recv,
                device_id={"fsdp": 2 * (index * RINGS + column(place)) + 1 - core},
                device_id_type=MESH,
            ).start()

    both_ways(0, start1)
    both_ways(0, start2_leaf)
    both_ways(1, start1)
    own_copy.wait()
    both_ways(0, start2)
    both_ways(0, short3)
    both_ways(1, start2_leaf)
    both_ways(0, long3)
    both_ways(0, short4)
    both_ways(1, start2)
    both_ways(0, long4)
    both_ways(1, short3)
    both_ways(1, long3)
    second_copy.wait()
    def in_turn(k):
        return 2 * lax.rem(k, 2) + lax.div(k, 2)

    each(4, lambda k: finish(in_turn(k)))
    both_ways(1, short4)
    both_ways(1, long4)
    each(FAR - 4, lambda k: finish(4 + in_turn(k)))
    finish_near(FAR)
    moment_copy = pltpu.make_async_copy(moment_v, moment, local_sem.at[3])
    moment_copy.start()

    def to_partner(source, target, send, recv):
        return pltpu.make_async_remote_copy(
            src_ref=source,
            dst_ref=target,
            send_sem=send,
            recv_sem=recv,
            device_id={"fsdp": partner},
            device_id_type=MESH,
        )

    def forward(place):
        here = gathered.at[core, place]
        pltpu.make_async_copy(here, here, row_recv.at[place]).wait()
        to_partner(here, here, pair_send, pair_recv).start()

    def send_adam(place):
        for index in range(COLS):
            to_owner(
                2 * (index * RINGS + column(place)) + core,
                sums_out.at[place, index],
                sums_in.at[chip],
                sum_send,
                sum_recv,
            )

    each(RINGS, send_adam)
    each(4, forward)
    each(FAR - 4, lambda k: forward(4 + in_turn(k)))

    stat_copy.wait()
    for place in range(FAR, RINGS):
        here = gathered.at[core, place]
        pltpu.make_async_copy(here, here, row_recv.at[place]).wait()
    near = gathered.at[1 - core, pl.ds(FAR, RINGS - FAR)]
    pltpu.make_async_copy(near, near, cross_recv).wait()
    there = gathered.at[1 - core, pl.ds(0, FAR)]
    pltpu.make_async_copy(there, there, pair_recv).wait()

    def assemble(place):
        source_z = lax.rem(z + RINGS - shift_of(place) + RINGS, RINGS)
        for index in range(COLS):
            pair = [gathered[c, place, index].astype(F32) for c in (0, 1)]
            start = pl.multiple_of((index * RINGS + source_z) * 16, 16)
            for c in range(4):
                both = [p[c * ROWS:(c + 1) * ROWS] for p in pair]
                block[pl.ds(start, 16), c * LANES:(c + 1) * LANES] = jnp.concatenate(both, axis=0).astype(BF16)

    each(8, assemble)

    @pl.when(core == 0)
    def _():
        p_f[...] = lax.dot_general(
            block[...], block[...], (((1,), (1,)), ((), ())), preferred_element_type=F32
        )

    @pl.when(core == 1)
    def _():
        p_f[...] = lax.dot_general(
            block[...], block[...], (((0,), (0,)), ((), ())), preferred_element_type=F32
        )

    def square_sum(value):
        return jnp.sum((value * value).reshape(value.shape[0] // ROWS, ROWS, value.shape[1]), axis=0)

    def halves(value):
        high = value.astype(BF16)
        return high, (value - high.astype(F32)).astype(BF16)

    def put(ref, here, value):
        high, low = halves(value)
        ref[(0,) + here] = high
        ref[(1,) + here] = low

    def three(left, right, rows, cols):
        def one(a, b):
            return jnp.dot(left[a, rows], right[b, :, cols], preferred_element_type=F32)

        return one(0, 0) + one(1, 0) + one(0, 1)

    low, high = slice(0, PART), slice(PART, SIZE)

    def product(left, right, use):
        def spread(piece, rows, cols):
            for t in range(0, PART, TILE):
                here = slice(rows.start + t, rows.start + t + TILE)
                use(here.start, cols, (here, cols), piece[t:t + TILE])

        corner = three(left, right, low, low)
        side = three(left, right, low, high)
        spread(corner, low, low)
        end = three(left, right, high, high)
        spread(side, low, high)
        spread(side.T, high, low)
        spread(end, high, high)

    def identity(t, cols, scale):
        shape = (TILE, cols.stop - cols.start)
        row = lax.broadcasted_iota(jnp.int32, shape, 0) + t
        lane = lax.broadcasted_iota(jnp.int32, shape, 1) + cols.start
        return jnp.where(row == lane, scale, 0.0)

    everything = slice(0, SIZE)
    norm = jnp.zeros((ROWS, SIZE), F32)
    for t in range(0, SIZE, TILE):
        here = slice(t, t + TILE)
        value = stat_decay * stat_v[here] + (1.0 - stat_decay) * p_f[here]
        a_f[here] = value
        norm = norm + square_sum(value)
        put(a_b, (here, everything), value)
    frobenius = jnp.sqrt(jnp.sum(norm, keepdims=True))
    scaling = 5.0 / (2.0 * frobenius)
    first = jnp.sqrt(jnp.sqrt(scaling))

    def squared(t, cols, here, q):
        value = (q * scaling) * scaling
        p_f[here] = value
        put(b_b, here, 0.0625 * value - (0.625 * scaling) * a_f[here])
        put(p_b, here, value)

    def cubed(t, cols, here, q):
        value = (1.5625 * scaling) * a_f[here] - 0.625 * p_f[here] + (0.0625 * scaling) * q
        n_f[here] = value
        put(n_b, here, value)

    def moved(t, cols, here, q):
        value = 1.5625 * n_f[here] + q
        m_f[here] = value
        put(m_b, here, value)

    def squared_again(t, cols, here, q):
        m = m_f[here]
        value = 1.25 * m - 0.25 * q
        n_f[here] = value
        put(n_b, here, value)
        put(b_b, here, 0.0625 * q - 0.625 * m)

    def fourth(t, cols, here, q):
        value = 1.5625 * n_f[here] + q
        p_f[here] = value
        put(p_b, here, value)

    steps_copy.wait()
    count = steps_v[0]

    def last_factor(t, cols, here, q):
        second_w = identity(t, cols, 1.25) - 0.25 * m_f[here]
        third = 1.25 * second_w - 0.25 * (1.5625 * p_f[here] + q)
        value = jnp.where(count == 2, second_w, third)
        n_f[here] = value
        put(n_b, here, value)

    def swap_half(h):
        here = roots.at[core, h]
        return to_partner(here, here, root_send.at[h], root_recv.at[h])

    def swapped_half(h):
        here = roots.at[1 - core, h]
        return to_partner(here, here, root_send.at[h], root_recv.at[h])

    def choose(t, cols, here, q):
        one = identity(t, cols, 1.25) - (0.25 * scaling) * a_f[here]
        more = 1.25 * n_f[here] - (0.25 * scaling) * q
        value = jnp.where(count == 1, one, more)
        h = cols.start // PART
        roots[core, h, t:t + TILE] = (first * value).astype(BF16)
        if t + TILE == SIZE:
            swap_half(h).start()

    product(a_b, a_b, squared)
    product(a_b, p_b, cubed)
    product(b_b, n_b, moved)
    product(m_b, m_b, squared_again)
    product(n_b, b_b, fourth)
    product(p_b, b_b, last_factor)

    for cols in (low, high):
        last = three(a_b, n_b, slice(0, SIZE), cols)
        for t in range(0, SIZE, TILE):
            choose(t, cols, (slice(t, t + TILE), cols), last[t:t + TILE])

    pltpu.make_async_copy(sums_in, sums_in, sum_recv).wait()
    adam_pair[core] = jnp.sum(sums_in[...], axis=0)
    adam_swap = to_partner(adam_pair.at[core], adam_pair.at[core], sum_pair_send, sum_pair_recv)
    adam_swapped = to_partner(adam_pair.at[1 - core], adam_pair.at[1 - core], sum_pair_send, sum_pair_recv)
    adam_swap.start()
    @pl.when(core == 1)
    def _():
        swapped_half(0).wait_recv()

    total = jnp.dot(roots[0, 0], block[0:PART], preferred_element_type=F32)

    @pl.when(core == 1)
    def _():
        swapped_half(1).wait_recv()

    total = total + jnp.dot(roots[0, 1], block[PART:SIZE], preferred_element_type=F32)
    middle[...] = total.astype(BF16)

    dir_sq = jnp.zeros((ROWS, PART), F32)
    for h in (0, 1):
        @pl.when(core == 0)
        def _():
            swapped_half(h).wait_recv()

        cols = slice(h * PART, (h + 1) * PART)
        q_f[:, cols] = jnp.dot(middle[...], roots[1, h], preferred_element_type=F32)
        for t in range(0, SIZE, TILE):
            here = slice(t, t + TILE)
            value = q_f[here, cols].astype(BF16).astype(F32)
            q_f[here, cols] = value
            dir_sq = dir_sq + square_sum(value)
    dir_sq = jnp.sum(dir_sq, keepdims=True)
    adam_swapped.wait_recv()
    adam_sq = jnp.sum(adam_pair[0] + adam_pair[1], keepdims=True)
    ratio = jnp.sqrt(adam_sq) / (jnp.sqrt(dir_sq) + ratio_eps)

    for t in range(PART // TILE):
        here = pl.ds(pl.multiple_of(core * PART + t * TILE, TILE), TILE)
        value = q_f[here] * ratio
        parts = [
            value[:, c * LANES:(c + 1) * LANES].reshape(TILE // ROWS, ROWS, LANES) for c in range(4)
        ]
        back[t * 8:(t + 1) * 8] = jnp.concatenate(parts, axis=1).astype(BF16)

    def give(row):
        for index in range(COLS):
            slot = 2 * (index // 2 * RINGS + row) + index % 2
            to_owner(core * HALF + slot, back.at[slot], upd.at[chip], back_send, back_recv)

    each(RINGS, give)

    for way in (0, 1):
        sent_raw = own.at[0]
        pltpu.make_async_copy(sent_raw, sent_raw, raw_send.at[way]).wait()
        pltpu.make_async_copy(codes_out.at[way], codes_out.at[way], code_send.at[way]).wait()
        pltpu.make_async_copy(units_out.at[way], units_out.at[way], unit_send.at[way]).wait()
    swap_half(0).wait_send()
    swap_half(1).wait_send()
    here = gathered.at[core, pl.ds(0, FAR)]
    pltpu.make_async_copy(here, here, pair_send).wait()
    here = gathered.at[core, pl.ds(0, RINGS - FAR)]
    pltpu.make_async_copy(here, here, cross_send).wait()
    sent = back.at[pl.ds(0, HALF - 1)]
    pltpu.make_async_copy(sent, sent, row_send).wait()
    sent_sums = sums_in.at[pl.ds(0, HALF - 1)]
    pltpu.make_async_copy(sent_sums, sent_sums, sum_send).wait()
    adam_swap.wait_send()
    moment_copy.wait()
    returns = lax.div(me, HALF) == core

    @pl.when(returns)
    def _():
        sent_back = back.at[pl.ds(0, HALF - 1)]
        pltpu.make_async_copy(sent_back, sent_back, back_send).wait()

    @pl.when(jnp.logical_not(returns))
    def _():
        pltpu.make_async_copy(back, back, back_send).wait()

    pltpu.make_async_copy(back, upd, back_recv).wait()


def write_out(upd, moment_in, update, moment, upd_v, update_v, moment_v, sems):
    def quarter(t):
        return pl.ds(t * 8, 8)

    def come(t):
        here = quarter(t)
        return (
            pltpu.make_async_copy(moment_in.at[here], moment_v.at[here], sems.at[t]),
            pltpu.make_async_copy(upd.at[here], upd_v.at[here], sems.at[4 + t]),
        )

    def go(t):
        here = quarter(t)
        return (
            pltpu.make_async_copy(moment_v.at[here], moment.at[here], sems.at[8 + t]),
            pltpu.make_async_copy(update_v.at[here], update.at[here], sems.at[12 + t]),
        )

    coming = [come(t) for t in range(4)]
    going = [go(t) for t in range(4)]
    for pair in coming:
        for copy in pair:
            copy.start()
    for t in range(4):
        coming[t][0].wait()
        going[t][0].start()
        coming[t][1].wait()
        wide = upd_v[t * 8:(t + 1) * 8].astype(F32)
        for c in range(4):
            update_v[t * 8:(t + 1) * 8, :, c * LANES:(c + 1) * LANES] = wide[:, c * ROWS:(c + 1) * ROWS].astype(BF16)
        going[t][1].start()
    for pair in going:
        for copy in pair:
            copy.wait()


def on_device(gradients, statistics, newton_steps, second_moment):
    chunk = (COLS, ROWS, SIZE)
    dma = pltpu.SemaphoreType.DMA
    square_f = pltpu.VMEM((SIZE, SIZE), F32)
    square_b = pltpu.VMEM((SIZE, SIZE), BF16)
    both = pltpu.VMEM((2, SIZE, SIZE), BF16)
    anywhere = pl.BlockSpec(memory_space=pl.ANY)
    group_f = pltpu.VMEM((COLS, RINGS, ROWS, SIZE), F32)
    upd, moment = pl.pallas_call(
        kernel,
        out_shape=(
            jax.ShapeDtypeStruct((HALF, 32, LANES), BF16),
            jax.ShapeDtypeStruct((COLS, RINGS, ROWS, SIZE), F32),
        ),
        in_specs=[anywhere] * 4,
        out_specs=(anywhere, anywhere),
        scratch_shapes=[
            pltpu.VMEM((WAYS, COLS, RINGS, ROWS, SIZE), BF16),
            square_f,
            group_f,
            group_f,
            pltpu.VMEM((2, 4) + chunk, BF16),
            pltpu.VMEM((2, 4) + chunk, BF16),
            pltpu.VMEM((2, 20) + chunk, jnp.int16),
            pltpu.VMEM((2, 20) + chunk, jnp.int16),
            pltpu.VMEM((2, 20, 2, 1, LANES), F32),
            pltpu.VMEM((2, 20, 2, 1, LANES), F32),
            pltpu.VMEM((66, 1, LANES), F32),
            pltpu.SMEM((1,), jnp.int32),
            pltpu.VMEM((RINGS, COLS, 32, LANES), BF16),
            pltpu.VMEM((2, RINGS, COLS, 32, LANES), BF16),
            pltpu.VMEM((RINGS, COLS, 1, LANES), F32),
            pltpu.VMEM((HALF, 1, LANES), F32),
            pltpu.VMEM((2, 1, LANES), F32),
            square_b,
            square_b,
            pltpu.VMEM((HALF, 32, LANES), BF16),
            pltpu.VMEM((2, 2, SIZE, PART), BF16),
        ]
        + [square_f] * 5
        + [both] * 5
        + [
            dma((5,)), dma((2,)), dma((2, 8)), dma((2,)), dma((2,)), dma((2, 20)), dma, dma((8,)), dma, dma,
            dma, dma, dma, dma, dma, dma, dma((2,)), dma((2,)), dma, dma,
        ],
        compiler_params=pltpu.CompilerParams(
            collective_id=0, has_side_effects=True, vmem_limit_bytes=56 * 2**20
        ),
    )(
        gradients.reshape(WAYS, COLS, RINGS, ROWS, SIZE),
        statistics.reshape(SIZE, SIZE),
        newton_steps,
        second_moment.reshape(COLS, RINGS, ROWS, SIZE),
    )
    return pl.pallas_call(
        write_out,
        out_shape=(
            jax.ShapeDtypeStruct((HALF, ROWS, SIZE), BF16),
            jax.ShapeDtypeStruct((HALF, ROWS, SIZE), F32),
        ),
        in_specs=[anywhere, anywhere],
        out_specs=(anywhere, anywhere),
        scratch_shapes=[
            pltpu.VMEM((HALF, 32, LANES), BF16),
            pltpu.VMEM((HALF, ROWS, SIZE), BF16),
            pltpu.VMEM((HALF, ROWS, SIZE), F32),
            dma((16,)),
        ],
    )(upd, moment.reshape(HALF, ROWS, SIZE))


def solution(mesh):
    return jax.shard_map(
        on_device,
        mesh=mesh,
        in_specs=(
            P("dp", None, "fsdp", None),
            P(("dp", "fsdp"), None, None),
            P(("dp", "fsdp")),
            P("dp", "fsdp", None),
        ),
        out_specs=(P("dp", "fsdp", None), P("dp", "fsdp", None)),
        check_vma=False,
    )
```
